512 devices in a mesh: leaf: 64 (over z, y), front: 8 (over x, core).
Axes of the slice: x: 4, y: 4, z: 16, core: 2. Of those that a mesh axis runs over, the one named last changes fastest.
Arguments:
- top_factor: float32 [1408, 2816], P('front', 'leaf'), may hold values from -1 to 3
- panel_two: float32 [1408, 5632], P('front', 'leaf'), may hold values from -0.109375 to 0.109375
- panel_three: float32 [1408, 11264], P('front', 'leaf'), may hold values from -0.109375 to 0.109375
- panel_four: float32 [1408, 22528], P('front', 'leaf'), may hold values from -0.109375 to 0.109375
- factor_two: float32 [1408, 5632], P('front', 'leaf'), may hold values from -1 to 3
- factor_three: float32 [1408, 11264], P('front', 'leaf'), may hold values from -1 to 3
- factor_four: float32 [1408, 22528], P('front', 'leaf'), may hold values from -1 to 3
Outputs:
- cov_one: float32 [1408, 2816], P('front', 'leaf')
- cross_two: float32 [1408, 5632], P('front', 'leaf')
- cov_two: float32 [1408, 5632], P('front', 'leaf')
- cross_three: float32 [1408, 11264], P('front', 'leaf')
- cov_three: float32 [1408, 11264], P('front', 'leaf')
- cross_four: float32 [1408, 22528], P('front', 'leaf')
- cov_four: float32 [1408, 22528], P('front', 'leaf')
The draws below stay inside these ranges and needn't reach their ends.
All inputs are finite; a program needn't handle non-finite values.
Results may differ from the reference program's by a relative error of at most 0.000088.
Values sent between devices are 32-bit elements; how exact they have to be, the bound alone decides.
No kernel may reach another device: no remote copies, remote signals or barrier semaphores. Data moves between devices by JAX's collectives and lax.ppermute only.
A program may use at most 64 MiB of HBM per device.

```python
import math
import jax
import jax.numpy as jnp
from jax import lax

S = 1408


def pivot_factor(key, node_count, scale_lo):
    gain_key, noise_key, column_key = jax.random.split(key, 3)
    row_index = jnp.arange(S)[:, None]
    column_index = jnp.arange(node_count * S)[None, :]
    diagonal = column_index % S == row_index
    diagonal_gain = jax.random.uniform(gain_key, (S, node_count * S), jnp.float32, 1.0, 2.0)
    column_scale = jnp.exp(jax.random.uniform(column_key, (1, node_count * S), jnp.float32, math.log(scale_lo), 1e-12))
    noise_part = jax.random.truncated_normal(noise_key, -4.0, 4.0, (S, node_count * S), jnp.float32) * (2.0 / math.sqrt(S))
    noise_part = jnp.clip(noise_part * column_scale, -0.95, 0.95)
    return jnp.where(diagonal, diagonal_gain, noise_part)


def draw_top_factor(key, part):
    key = jax.random.fold_in(key, 11)
    return pivot_factor(key, 2, 1.0)


def draw_factor_two(key, part):
    key = jax.random.fold_in(key, 12)
    return pivot_factor(key, 4, 1.0)


def draw_factor_three(key, part):
    key = jax.random.fold_in(key, 13)
    return pivot_factor(key, 8, 1.0)


def draw_factor_four(key, part):
    key = jax.random.fold_in(key, 14)
    return pivot_factor(key, 16, 1.0)


def levels(rng, extent, pieces, low, largest):
    factor_of, own = 1.0, jax.random.fold_in(rng, 6)
    for dim, shards_of in pieces:
        steps = jnp.exp(jax.random.uniform(jax.random.fold_in(own, dim), (shards_of,), jnp.float32, low / len(pieces), largest / len(pieces)))
        factor_of = factor_of * jnp.repeat(steps, extent[dim] // shards_of).reshape([-1 if axis == dim else 1 for axis in range(len(extent))])
    return factor_of


def scatter_about(stream_key, dims, deviation, bound, cuts=(), kind=jnp.bfloat16):
    result = jax.random.normal(stream_key, dims, jnp.float32) * deviation
    if len(cuts) > 0:
        result = levels(stream_key, dims, cuts, -0.22, 0.18) * result
    return jnp.clip(result, min=-bound, max=bound).astype(kind)


def setup_inputs(seed: int = 0) -> dict:
    arg_keys = jax.random.split(jax.random.key(seed), 8)
    return {
        "top_factor": draw_top_factor(jax.random.fold_in(arg_keys[7], 71), 0),
        "panel_two": scatter_about(arg_keys[1], (S, 4 * S), (2 * S) ** -0.5, 0.109375, ((0, 8), (1, 64)), jnp.float32),
        "panel_three": scatter_about(arg_keys[2], (S, 8 * S), (2 * S) ** -0.5, 0.109375, ((0, 8), (1, 64)), jnp.float32),
        "panel_four": scatter_about(arg_keys[3], (S, 16 * S), (2 * S) ** -0.5, 0.109375, ((0, 8), (1, 64)), jnp.float32),
        "factor_two": draw_factor_two(jax.random.fold_in(arg_keys[7], 71), 0),
        "factor_three": draw_factor_three(jax.random.fold_in(arg_keys[7], 71), 0),
        "factor_four": draw_factor_four(jax.random.fold_in(arg_keys[7], 71), 0),
    }


def gram_blocks(factor):
    blocks = factor.reshape(S, -1, S)
    return jnp.einsum('kni,knj->inj', blocks, blocks, precision=lax.Precision.HIGHEST).reshape(S, -1)


def descend(parent_cov, panel_tile, factor_tile):
    node_count = panel_tile.shape[1] // S
    parent_blocks = jnp.repeat(parent_cov.reshape(S, -1, S), 2, axis=1)
    panel_blocks = panel_tile.reshape(S, node_count, S)
    cross_blocks = -jnp.einsum('ink,knj->inj', parent_blocks, panel_blocks, precision=lax.Precision.HIGHEST)
    factor_blocks = factor_tile.reshape(S, node_count, S)
    gram_part = jnp.einsum('kni,knj->inj', factor_blocks, factor_blocks, precision=lax.Precision.HIGHEST)
    coupled = jnp.einsum('kni,knj->inj', panel_blocks, cross_blocks, precision=lax.Precision.HIGHEST)
    return cross_blocks.reshape(S, -1), (gram_part - coupled).reshape(S, -1)


def reference(top_factor, panel_two, panel_three, panel_four, factor_two, factor_three, factor_four):
    cov_one = gram_blocks(top_factor)
    cross_two, cov_two = descend(cov_one, panel_two, factor_two)
    cross_three, cov_three = descend(cov_two, panel_three, factor_three)
    cross_four, cov_four = descend(cov_three, panel_four, factor_four)
    return (cov_one, cross_two, cov_two, cross_three, cov_three, cross_four, cov_four)
```

```python
import jax
import jax.numpy as jnp
from jax import lax
from jax.sharding import PartitionSpec as P

Y = 4
CORES = 2


def dot(first, second):
    return jnp.dot(
        first, second, precision=lax.Precision.HIGH, preferred_element_type=jnp.float32
    )


def dot_nt(first, second):
    return lax.dot_general(
        first,
        second,
        (((1,), (1,)), ((), ())),
        precision=lax.Precision.HIGH,
        preferred_element_type=jnp.float32,
    )


def local(top_factor, panel_two, panel_three, panel_four, factor_two, factor_three, factor_four):
    leaves = lax.axis_size("leaf")
    fronts = lax.axis_size("front")
    share = top_factor.shape[0]
    size = share * fronts
    width = panel_four.shape[1]
    xs = fronts // CORES
    leaf = lax.axis_index("leaf")
    front = lax.axis_index("front")
    z, x, core = leaf // Y, front // CORES, front % CORES
    y_groups = [list(range(i, i + Y)) for i in range(0, leaves, Y)]

    def from_plane(value, distance):
        pairs = [(i, ((i // Y) ^ distance) * Y + i % Y) for i in range(leaves)]
        return lax.ppermute(value, "leaf", pairs)

    def from_core(value):
        return lax.ppermute(value, "front", [(i, i ^ 1) for i in range(fronts)])

    def shift_x(value, distance):
        pairs = [
            (i, (i // CORES + distance) % xs * CORES + i % CORES) for i in range(fronts)
        ]
        return lax.ppermute(value, "front", pairs)

    def joined(own, partner, distance):
        upper = (z // distance) % 2 == 1
        axis = own.ndim - 2
        return jnp.where(
            upper, jnp.stack([partner, own], axis), jnp.stack([own, partner], axis)
        )

    def exchange(values, distance):
        flat = [value.reshape(-1, share) for value in values]
        rows = [value.shape[0] for value in flat]
        got = from_plane(jnp.concatenate(flat, 0), distance)
        out, at = [], 0
        for value, count in zip(values, rows):
            out.append(joined(value, got[at : at + count].reshape(value.shape), distance))
            at += count
        return out

    def plane_rows(tiles):
        got = lax.all_gather(
            jnp.stack(tiles), "leaf", axis=0, axis_index_groups=y_groups
        )
        return [got[:, i] for i in range(len(tiles))]

    def natural_rows(gathered, planes):
        by_plane = gathered.reshape(Y, planes, -1, share)
        return jnp.swapaxes(by_plane, 0, 1).reshape(xs, CORES, share, share)

    def front_sum(term_fn):
        other = from_core(term_fn(1 - core))
        both = (term_fn(core) + other).reshape(xs, share, width)
        total = lax.dynamic_index_in_dim(both, x, 0, False)
        for distance in (1, 3, 2):
            piece = lax.dynamic_index_in_dim(both, (x + distance) % xs, 0, False)
            total = total + shift_x(piece, distance)
        return total

    def half(rows, which):
        picked = lax.dynamic_index_in_dim(rows, which, 1, False)
        return picked.reshape(xs * share, share)

    f1 = joined(top_factor.T, from_plane(top_factor.T, 4), 4)
    f1, p2, f2 = exchange([f1, panel_two.T, factor_two.T], 2)
    (f1,) = exchange([f1], 1)
    p2, f2, p3, f3 = exchange([p2, f2, panel_three.T, factor_three.T], 1)
    f1, p2, f2, p3, f3 = (v.reshape(width, share) for v in (f1, p2, f2, p3, f3))
    p4, f4 = panel_four.T, factor_four.T

    (rows,) = plane_rows([f1])
    rows = natural_rows(rows, 8)
    parent = front_sum(lambda which: dot_nt(half(rows, which), f1))
    parent_planes = 8

    def own(value, planes):
        part = width // planes
        return lax.dynamic_slice_in_dim(value, (z % planes) * part, part, 1)

    results = [own(parent, 8)]
    panels = jnp.concatenate([p2.T, p3.T, p4.T], 1)
    panels = lax.all_gather(panels, "front", axis=0, tiled=True)
    p2_rows, f2_rows = plane_rows([p2, f2])
    p3_rows, f3_rows, p4_rows, f4_rows = plane_rows([p3, f3, p4, f4])
    levels = ((4, f2, p2_rows, f2_rows), (2, f3, p3_rows, f3_rows), (1, f4, p4_rows, f4_rows))
    for level, (planes, factor, p_rows, f_rows) in enumerate(levels):
        columns = panels[:, level * width : (level + 1) * width]
        columns = columns.reshape(parent_planes, Y, -1, width)
        columns = jnp.swapaxes(columns, 0, 1).reshape(Y, width, width)
        p_rows = natural_rows(p_rows, planes)
        f_rows = natural_rows(f_rows, planes)
        parent_rows = lax.all_gather(
            parent, "leaf", axis=0, axis_index_groups=y_groups
        )
        product = sum(dot(parent_rows[i], columns[i]) for i in range(Y))

        def term(which):
            return dot(half(p_rows, which), product) + dot_nt(half(f_rows, which), factor)

        parent = front_sum(term)
        parent_planes = planes
        results.append(own(-product, planes))
        results.append(own(parent, planes))
    return tuple(results)


def solution(mesh):
    spec = P("front", "leaf")
    return jax.shard_map(
        local, mesh=mesh, in_specs=(spec,) * 7, out_specs=(spec,) * 7, check_vma=False
    )
```

```python
import functools

import jax
import jax.numpy as jnp
from jax import lax
from jax.experimental import pallas as pl
from jax.experimental.pallas import tpu as pltpu
from jax.sharding import PartitionSpec as P

Y = 4
XS = 4
CORES = 2
VMEM_BYTES = 48 * 1024 * 1024


def split(value):
    high = value.astype(jnp.bfloat16)
    low = (value - high.astype(jnp.float32)).astype(jnp.bfloat16)
    return high, low


def product(first, second):
    (fh, fl), (sh, sl) = first, second
    run = functools.partial(jnp.dot, preferred_element_type=jnp.float32)
    return run(fh, sh) + (run(fh, sl) + run(fl, sh))


def join(where_ref, own_ref, got_ref, p4_ref, f4_ref, f1_ref, rows_ref, p2_ref, columns_ref):
    z = where_ref[2]
    pieces = []
    for plane in range(8):
        distance = plane ^ z
        at, far = ((distance >> 1) & 1) * 3 + 2, (distance >> 2) == 1
        both = jnp.where((distance & 1) == 0, own_ref[at], got_ref[at])
        pieces.append(jnp.where(far, both[44:], both[:44]))
    f1_ref[...] = jnp.concatenate(pieces, 0).T
    for which in range(2):
        pieces = []
        for plane in range(4):
            distance = plane ^ (z % 4)
            at = (distance >> 1) * 3 + which
            pieces.append(jnp.where((distance & 1) == 0, own_ref[at], got_ref[at]))
        tile = jnp.concatenate(pieces, 0).T
        rows_ref[which] = tile
        if which == 0:
            p2_ref[...] = tile
    for which in range(2):
        pieces = []
        for plane in range(2):
            near = plane == (z % 2)
            for at in (6 + 2 * which, 7 + 2 * which):
                pieces.append(jnp.where(near, own_ref[at], got_ref[at]))
        tile = jnp.concatenate(pieces, 0).T
        rows_ref[2 + which] = tile
        if which == 0:
            columns_ref[0] = tile
    rows_ref[4] = p4_ref[...]
    rows_ref[5] = f4_ref[...]
    columns_ref[1] = p4_ref[...]


def share_terms(where_ref, planes, tiles, factors, other_ref, mine_ref):
    x, core = where_ref[0], where_ref[1]
    width = factors[0][0].shape[1] // planes
    step = min(width, 176)
    for y in range(Y):
        total = None
        for tile, factor in zip(tiles, factors):
            term = product(split(tile(y).T), factor)
            total = term if total is None else total + term
        for plane in range(planes):
            for part in range(0, width, step):
                column = (plane * Y + y) * width + part
                block, offset = column // 176, column % 176
                value = total[plane * width + part : plane * width + part + step]
                at = (block // CORES - x) % XS
                same = core == (block % CORES)

                @pl.when(same)
                def _():
                    mine_ref[at, offset : offset + step, :] = value

                @pl.when(jnp.logical_not(same))
                def _():
                    other_ref[at, offset : offset + step, :] = value


def top_terms(where_ref, rows_ref, own_ref, other_ref, mine_ref):
    factors = [split(own_ref[...])]
    share_terms(where_ref, 8, [lambda y: rows_ref[y]], factors, other_ref, mine_ref)


def level_terms(planes, where_ref, parent_ref, *refs):
    *column_refs, rows_ref, own_ref, cross_ref, other_ref, mine_ref = refs
    x, core = where_ref[0], where_ref[1]
    parts, width = planes * 2, own_ref.shape[-1] // (planes * 2)

    def columns(start, count):
        block, offset = start // 176, start % 176
        if len(column_refs) == 1:
            return column_refs[0][block, 0, offset : offset + count, :]
        step = (block // CORES - x) % XS
        same = core == (block % CORES)
        mine = column_refs[0][step, offset : offset + count, :]
        theirs = column_refs[1][step, offset : offset + count, :]
        return jnp.where(same, mine, theirs)

    total = None
    for y in range(Y):
        rows = [columns((p * Y + y) * width, width) for p in range(parts)]
        term = product(split(parent_ref[y]), split(jnp.concatenate(rows, 0)))
        total = term if total is None else total + term
    cross_ref[...] = -total
    tiles = [lambda y: rows_ref[y, 0], lambda y: rows_ref[y, 1]]
    factors = [split(total), split(own_ref[0])]
    share_terms(where_ref, planes, tiles, factors, other_ref, mine_ref)


def add_pieces(mine_ref, got_ref, *out_refs):
    for step, out_ref in enumerate(out_refs):
        out_ref[...] = mine_ref[step] + got_ref[step]


def local(top_factor, panel_two, panel_three, panel_four, factor_two, factor_three, factor_four):
    leaves = lax.axis_size("leaf")
    fronts = lax.axis_size("front")
    share = top_factor.shape[0]
    width = panel_four.shape[1]
    leaf = lax.axis_index("leaf")
    front = lax.axis_index("front")
    z, x, core = leaf // Y, front // CORES, front % CORES
    where = jnp.stack([x, core, z % 8]).astype(jnp.int32)
    y_groups = [list(range(i, i + Y)) for i in range(0, leaves, Y)]

    def from_plane(value, distance):
        pairs = [(i, ((i // Y) ^ distance) * Y + i % Y) for i in range(leaves)]
        return lax.ppermute(value, "leaf", pairs)

    def from_core(value):
        return lax.ppermute(value, "front", [(i, i ^ 1) for i in range(fronts)])

    def shift_x(value, distance):
        pairs = [
            (i, (i // CORES + distance) % XS * CORES + i % CORES) for i in range(fronts)
        ]
        return lax.ppermute(value, "front", pairs)

    def y_gather(value):
        return lax.all_gather(value, "leaf", axis=0, axis_index_groups=y_groups)

    tile = jax.ShapeDtypeStruct((share, width), jnp.float32)
    tiles = jax.ShapeDtypeStruct((XS, share, width), jnp.float32)
    scalars = pl.BlockSpec(memory_space=pltpu.SMEM)

    def full(value):
        return pl.BlockSpec(value.shape, lambda i: (0,) * len(value.shape))

    def call(kernel, out_shape, in_specs, flops, *args):
        many = isinstance(out_shape, (tuple, list))
        specs = [full(o) for o in (out_shape if many else [out_shape])]
        return pl.pallas_call(
            kernel,
            out_shape=out_shape,
            grid=(1,),
            in_specs=in_specs,
            out_specs=specs if many else specs[0],
            compiler_params=pltpu.CompilerParams(vmem_limit_bytes=VMEM_BYTES),
            cost_estimate=pl.CostEstimate(
                flops=flops, bytes_accessed=8_000_000, transcendentals=0
            ),
        )(*args)

    def front_total(other, mine):
        got = from_core(other)
        pieces = call(add_pieces, [tile] * XS, [full(tiles)] * 2, 1_000_000, mine, got)
        total = pieces[0]
        for distance in (1, 3, 2):
            total = total + shift_x(pieces[distance], distance)
        return total

    half = share // 2
    first = top_factor.T
    stack = functools.partial(jax.ShapeDtypeStruct, dtype=jnp.float32)

    def turn(p2_ref, f2_ref, p3_ref, f3_ref, own_ref, got_ref, two_ref, three_ref):
        two_ref[0] = p2_ref[...].T
        two_ref[1] = f2_ref[...].T
        two_ref[2] = jnp.concatenate([own_ref[...], got_ref[...]], 0)
        for which, ref in enumerate((p3_ref, f3_ref)):
            turned = ref[...].T
            for part in range(2):
                three_ref[2 * which + part] = turned[part * half : (part + 1) * half]

    raw = [panel_two, factor_two, panel_three, factor_three, first, from_plane(first, 4)]
    two, three = call(
        turn,
        [stack((3, half, share)), stack((4, half, share))],
        [full(v) for v in raw],
        1_000_000,
        *raw,
    )
    near = jnp.concatenate([two, from_plane(two, 2), three], 0)
    got = from_plane(near, 1)
    f1, deep, p2, columns_in = call(
        join,
        [tile, stack((6, share, width)), tile, stack((2, share, width))],
        [scalars, full(near), full(got), full(tile), full(tile)],
        1_000_000,
        where,
        near,
        got,
        panel_four,
        factor_four,
    )
    rows = y_gather(deep)
    panels = lax.all_gather(columns_in, "front", axis=0)
    near = jnp.stack([p2] + [shift_x(p2, (XS - d) % XS) for d in range(1, XS)])
    far = from_core(near)

    work = 6 * share * share * XS * width
    other, mine = call(
        top_terms,
        [tiles, tiles],
        [scalars, full(tiles), full(tile)],
        2 * work,
        where,
        y_gather(f1),
        f1,
    )
    parent = front_total(other, mine)

    def own(value, planes):
        part = width // planes
        return lax.dynamic_slice_in_dim(value, (z % planes) * part, part, 1)

    results = [own(parent, 8)]
    for level, planes in enumerate((4, 2, 1)):
        row_spec = pl.BlockSpec((Y, 2, share, width), lambda i, n=level: (0, n, 0, 0))
        own_spec = pl.BlockSpec((1, share, width), lambda i, n=level: (2 * n + 1, 0, 0))
        if level == 0:
            columns, column_specs = [near, far], [full(tiles)] * 2
        else:
            columns = [panels]
            column_specs = [
                pl.BlockSpec((fronts, 1, share, width), lambda i, n=level: (0, n - 1, 0, 0))
            ]
        cross, other, mine = call(
            functools.partial(level_terms, planes),
            [tile, tiles, tiles],
            [scalars, full(tiles), *column_specs, row_spec, own_spec],
            4 * work,
            where,
            y_gather(parent),
            *columns,
            rows,
            deep,
        )
        parent = front_total(other, mine)
        results.append(own(cross, planes))
        results.append(own(parent, planes))
    return tuple(results)


def solution(mesh):
    spec = P("front", "leaf")
    return jax.shard_map(
        local, mesh=mesh, in_specs=(spec,) * 7, out_specs=(spec,) * 7, check_vma=False
    )
```

```python
import functools

import jax
import jax.numpy as jnp
from jax import lax
from jax.experimental import pallas as pl
from jax.experimental.pallas import tpu as pltpu
from jax.sharding import PartitionSpec as P

Y = 4
XS = 4
CORES = 2
VMEM_BYTES = 48 * 1024 * 1024


def split(value):
    high = value.astype(jnp.bfloat16)
    low = (value - high.astype(jnp.float32)).astype(jnp.bfloat16)
    return high, low


def product(first, second):
    (fh, fl), (sh, sl) = first, second
    run = functools.partial(jnp.dot, preferred_element_type=jnp.float32)
    return run(fh, sh) + (run(fh, sl) + run(fl, sh))


def block_of(ref, index):
    return ref[:, index * 176 : (index + 1) * 176]


def turn(p2_ref, f2_ref, own_ref, got_ref, out_ref):
    top = jnp.concatenate([own_ref[...], got_ref[...]], 0)
    out_ref[...] = jnp.concatenate([p2_ref[...].T, f2_ref[...].T, top], 1)


def pack(two_ref, got_ref, p3_ref, f3_ref, out_ref):
    parts = [two_ref[...], got_ref[...]]
    for ref in (p3_ref, f3_ref):
        turned = ref[...].T
        parts += [turned[:88], turned[88:]]
    out_ref[...] = jnp.concatenate(parts, 1)


def join(where_ref, own_ref, got_ref, panels_ref, f1_ref, rows_ref):
    del panels_ref
    z = where_ref[2]

    def at(which, distance):
        far = ((distance >> 1) & 1) == 1
        own = jnp.where(far, block_of(own_ref, which + 3), block_of(own_ref, which))
        got = jnp.where(far, block_of(got_ref, which + 3), block_of(got_ref, which))
        return jnp.where((distance & 1) == 1, got, own)

    pieces = []
    for plane in range(8):
        distance = plane ^ z
        both = at(2, distance)
        pieces.append(jnp.where((distance >> 2) == 1, both[44:], both[:44]))
    f1_ref[...] = jnp.concatenate(pieces, 0).T
    for which in range(2):
        pieces = [at(which, plane ^ (z % 4)) for plane in range(4)]
        rows_ref[which] = jnp.concatenate(pieces, 0).T
    for which in range(2):
        pieces = []
        for plane in range(2):
            near = plane == (z % 2)
            for index in (6 + 2 * which, 7 + 2 * which):
                pieces.append(
                    jnp.where(near, block_of(own_ref, index), block_of(got_ref, index))
                )
        rows_ref[2 + which] = jnp.concatenate(pieces, 0).T


def share_terms(where_ref, planes, tiles, factors, other_ref, mine_ref):
    x, core = where_ref[0], where_ref[1]
    width = tiles[0](0).shape[1] // planes
    step = min(width, 176)
    for y in range(Y):
        total = None
        for tile, factor in zip(tiles, factors):
            term = product(split(tile(y).T), factor)
            total = term if total is None else total + term
        for plane in range(planes):
            for part in range(0, width, step):
                column = (plane * Y + y) * width + part
                block, offset = column // 176, column % 176
                value = total[plane * width + part : plane * width + part + step]
                at = (block // CORES - x) % XS
                same = core == (block % CORES)

                @pl.when(same)
                def _():
                    mine_ref[at, offset : offset + step, :] = value

                @pl.when(jnp.logical_not(same))
                def _():
                    other_ref[at, offset : offset + step, :] = value


def top_terms(where_ref, rows_ref, own_ref, p4_ref, f4_ref, other_ref, mine_ref, last_ref):
    factors = [split(own_ref[...])]
    share_terms(where_ref, 8, [lambda y: rows_ref[y]], factors, other_ref, mine_ref)
    last_ref[0] = p4_ref[...]
    last_ref[1] = f4_ref[...]


def level_terms(planes, where_ref, parent_ref, columns_ref, rows_ref, own_ref, *out_refs):
    cross_ref, other_ref, mine_ref = out_refs
    z, count = where_ref[2], own_ref.shape[1]
    total = None
    for y in range(Y):
        if planes == 4:
            left = parent_ref[y]
            parts = [
                columns_ref[p, y * 44 : (y + 1) * 44, :count] for p in range(8)
            ]
        elif planes == 2:
            left = parent_ref[4 * y : 4 * y + 4].reshape(352, 176).T
            low = (y % 2) * 88
            parts = []
            for q in range(4):
                p = (z % 4) ^ ((q & 1) * 2 + (q >> 1))
                parts.append(columns_ref[p * 2 + y // 2, low : low + 88, :count])
        else:
            left = parent_ref[2 * y : 2 * y + 2].reshape(352, 176).T
            parts = [columns_ref[((z % 2) ^ q) * Y + y, :, :count] for q in range(2)]
        term = product(split(left), split(jnp.concatenate(parts, 0)))
        total = term if total is None else total + term
    cross_ref[...] = -total
    tiles = [lambda y: rows_ref[y, 0], lambda y: rows_ref[y, 1]]
    factors = [split(total), split(own_ref[...])]
    share_terms(where_ref, planes, tiles, factors, other_ref, mine_ref)


def finish(*refs):
    *in_refs, out_ref, turned_ref = refs
    total = sum(ref[...] for ref in in_refs)
    out_ref[...] = total
    turned_ref[...] = total.T


def add_pieces(mine_ref, got_ref, *out_refs):
    for step, out_ref in enumerate(out_refs):
        out_ref[...] = mine_ref[step] + got_ref[step]


def local(top_factor, panel_two, panel_three, panel_four, factor_two, factor_three, factor_four):
    leaves = lax.axis_size("leaf")
    fronts = lax.axis_size("front")
    share = top_factor.shape[0]
    width = panel_four.shape[1]
    leaf = lax.axis_index("leaf")
    front = lax.axis_index("front")
    z, x, core = leaf // Y, front // CORES, front % CORES
    where = jnp.stack([x, core, z % 8]).astype(jnp.int32)
    y_groups = [list(range(i, i + Y)) for i in range(0, leaves, Y)]

    def from_plane(value, distance):
        pairs = [(i, ((i // Y) ^ distance) * Y + i % Y) for i in range(leaves)]
        return lax.ppermute(value, "leaf", pairs)

    def from_core(value):
        return lax.ppermute(value, "front", [(i, i ^ 1) for i in range(fronts)])

    def shift_x(value, distance):
        pairs = [
            (i, (i // CORES + distance) % XS * CORES + i % CORES) for i in range(fronts)
        ]
        return lax.ppermute(value, "front", pairs)

    def y_gather(value):
        return lax.all_gather(value, "leaf", axis=0, axis_index_groups=y_groups)

    stack = functools.partial(jax.ShapeDtypeStruct, dtype=jnp.float32)
    tile, tiles = stack((share, width)), stack((XS, share, width))
    scalars = pl.BlockSpec(memory_space=pltpu.SMEM)

    def full(value):
        return pl.BlockSpec(value.shape, lambda i: (0,) * len(value.shape))

    def call(kernel, out_shape, in_specs, flops, *args):
        many = isinstance(out_shape, (tuple, list))
        specs = [full(o) for o in (out_shape if many else [out_shape])]
        return pl.pallas_call(
            kernel,
            out_shape=out_shape,
            grid=(1,),
            in_specs=in_specs,
            out_specs=specs if many else specs[0],
            compiler_params=pltpu.CompilerParams(vmem_limit_bytes=VMEM_BYTES),
            cost_estimate=pl.CostEstimate(
                flops=flops, bytes_accessed=8_000_000, transcendentals=0
            ),
        )(*args)

    def front_total(other, mine):
        got = from_core(other)
        piece = stack(mine.shape[1:])
        pieces = call(
            add_pieces, [piece] * XS, [full(mine), full(got)], 1_000_000, mine, got
        )
        parts = [pieces[0]] + [shift_x(pieces[d], d) for d in (1, 3, 2)]
        turned = stack(piece.shape[::-1])
        return call(finish, [piece, turned], [full(piece)] * XS, 1_000_000, *parts)

    def padded(value):
        return jnp.pad(value, ((0, 0), (0, -value.shape[1] % 128)))

    panels = jnp.concatenate([padded(panel_four), padded(panel_two), padded(panel_three)], 1)
    panels = lax.all_gather(panels, "front", axis=0)

    half = share // 2
    first = top_factor.T
    raw = [panel_two, factor_two, first, from_plane(first, 4)]
    two = call(turn, stack((half, 3 * share)), [full(v) for v in raw], 1_000_000, *raw)
    raw = [two, from_plane(two, 2), panel_three, factor_three]
    near = call(pack, stack((half, 10 * share)), [full(v) for v in raw], 1_000_000, *raw)
    f1, deep = call(
        join,
        [tile, stack((4, share, width))],
        [scalars, full(near), full(near), pl.BlockSpec(memory_space=pl.ANY)],
        1_000_000,
        where,
        near,
        from_plane(near, 1),
        panels,
    )
    rows = y_gather(deep)

    work = 6 * share * share * XS * width
    other, mine, last = call(
        top_terms,
        [tiles, tiles, stack((2, share, width))],
        [scalars, full(tiles), full(tile), full(tile), full(tile)],
        2 * work,
        where,
        y_gather(f1),
        f1,
        panel_four,
        factor_four,
    )
    last_rows = y_gather(last)
    parent, _ = front_total(other, mine)
    part = width // 8
    results = [lax.dynamic_slice_in_dim(parent, (z % 8) * part, part, 1)]

    shifts = {4: (), 2: (2, 1), 1: (1,)}
    for planes, factor, lanes, at in (
        (4, factor_two, 128, 3),
        (2, factor_three, 256, 2),
        (1, factor_four, 384, 0),
    ):
        if planes < 4:
            parent = parent[None]
        for distance in shifts[planes]:
            parent = jnp.concatenate([parent, from_plane(parent, distance)], 0)
        gathered = y_gather(parent)
        if planes < 4:
            gathered = gathered.reshape(-1, *gathered.shape[2:])
        count = factor.shape[1]
        level = 0 if planes == 4 else 1 if planes == 2 else 0
        source = last_rows if planes == 1 else rows
        cross, other, mine = call(
            functools.partial(level_terms, planes),
            [stack((share, count)), stack((XS, share, count)), stack((XS, share, count))],
            [
                scalars,
                full(gathered),
                pl.BlockSpec((fronts, share, lanes), lambda i, n=at: (0, 0, n)),
                pl.BlockSpec((Y, 2, share, width), lambda i, n=level: (0, n, 0, 0)),
                full(factor),
            ],
            4 * work // planes,
            where,
            gathered,
            panels,
            source,
            factor,
        )
        covariance, parent = front_total(other, mine)
        results.append(cross)
        results.append(covariance)
    return tuple(results)


def solution(mesh):
    spec = P("front", "leaf")
    return jax.shard_map(
        local, mesh=mesh, in_specs=(spec,) * 7, out_specs=(spec,) * 7, check_vma=False
    )
```

```python
import functools

import jax
import jax.numpy as jnp
from jax import lax
from jax.experimental import pallas as pl
from jax.experimental.pallas import tpu as pltpu
from jax.sharding import PartitionSpec as P

Y = 4
XS = 4
CORES = 2
VMEM_BYTES = 48 * 1024 * 1024


def split(value):
    high = value.astype(jnp.bfloat16)
    low = (value - high.astype(jnp.float32)).astype(jnp.bfloat16)
    return high, low


def product(first, second):
    (fh, fl), (sh, sl) = first, second
    run = functools.partial(jnp.dot, preferred_element_type=jnp.float32)
    return run(fh, sh) + (run(fh, sl) + run(fl, sh))


def block_of(ref, index):
    return ref[:, index * 176 : (index + 1) * 176]


def turn(f2_ref, own_ref, got_ref, out_ref):
    top = jnp.concatenate([own_ref[...], got_ref[...]], 0)
    out_ref[...] = jnp.concatenate([f2_ref[...].T, top], 1)


def pack(two_ref, got_ref, p3_ref, f3_ref, out_ref):
    parts = [two_ref[...], got_ref[...]]
    for ref in (p3_ref, f3_ref):
        turned = ref[...].T
        parts += [turned[:88], turned[88:]]
    out_ref[...] = jnp.concatenate(parts, 1)


def join(where_ref, own_ref, got_ref, panels_ref, f1_ref, rows_ref, p3_ref):
    del panels_ref
    z = where_ref[2]

    def at(which, distance):
        far = ((distance >> 1) & 1) == 1
        own = jnp.where(far, block_of(own_ref, which + 2), block_of(own_ref, which))
        got = jnp.where(far, block_of(got_ref, which + 2), block_of(got_ref, which))
        return jnp.where((distance & 1) == 1, got, own)

    pieces = []
    for plane in range(8):
        distance = plane ^ z
        both = at(1, distance)
        pieces.append(jnp.where((distance >> 2) == 1, both[44:], both[:44]))
    f1_ref[...] = jnp.concatenate(pieces, 0).T
    pieces = [at(0, plane ^ (z % 4)) for plane in range(4)]
    rows_ref[0] = jnp.concatenate(pieces, 0).T
    for which in range(2):
        pieces = []
        for plane in range(2):
            near = plane == (z % 2)
            for index in (4 + 2 * which, 5 + 2 * which):
                pieces.append(
                    jnp.where(near, block_of(own_ref, index), block_of(got_ref, index))
                )
        tile = jnp.concatenate(pieces, 0).T
        if which == 0:
            p3_ref[...] = tile
        else:
            rows_ref[1] = tile


def share_terms(where_ref, planes, turned, factors, first, other_ref, mine_ref):
    x, core = where_ref[0], where_ref[1]
    last = first + factors[0][0].shape[1]
    for y in range(Y):
        total = None
        for tile, factor in zip(turned, factors):
            term = product(split(tile(y)), factor)
            total = term if total is None else total + term
        width = total.shape[0] // planes
        step = min(width, 176)
        for plane in range(planes):
            for part in range(0, width, step):
                column = (plane * Y + y) * width + part
                block, offset = column // 176, column % 176
                value = total[plane * width + part : plane * width + part + step]
                at = (block // CORES - x) % XS
                same = core == (block % CORES)

                @pl.when(same)
                def _():
                    mine_ref[at, offset : offset + step, first:last] = value

                @pl.when(jnp.logical_not(same))
                def _():
                    other_ref[at, offset : offset + step, first:last] = value


def times_columns(planes, z, left, columns_ref, count):
    total = None
    for y in range(Y):
        if planes == 4:
            parts = [
                columns_ref[p, y * 44 : (y + 1) * 44, :count] for p in range(8)
            ]
        elif planes == 2:
            low = (y % 2) * 88
            parts = []
            for q in range(4):
                p = (z % 4) ^ ((q & 1) * 2 + (q >> 1))
                parts.append(columns_ref[p * 2 + y // 2, low : low + 88, :count])
        else:
            parts = [columns_ref[((z % 2) ^ q) * Y + y, :, :count] for q in range(2)]
        term = product(split(left(y)), split(jnp.concatenate(parts, 0)))
        total = term if total is None else total + term
    return total


def top_product(where_ref, rows_ref, columns_ref, *refs):
    *in_refs, out_ref, turned_ref, last_ref = refs
    count = out_ref.shape[1]
    total = times_columns(4, where_ref[2], lambda y: rows_ref[y], columns_ref, count)
    out_ref[...] = total
    turned_ref[...] = total.T
    for index, ref in enumerate(in_refs):
        last_ref[index] = ref[...]


def top_terms(where_ref, f1_rows_ref, f1_ref, a_ref, a_rows_ref, f2_rows_ref, f2_ref, *refs):
    p4_ref, other_ref, mine_ref, last_ref = refs
    last_ref[...] = p4_ref[...]
    z = where_ref[2]

    def a_turned(y):
        pieces = []
        for plane in range(4):
            distance = plane ^ (z % 4)
            pieces.append(a_rows_ref[y * 4 + (distance >> 1) + (distance & 1) * 2])
        return jnp.concatenate(pieces, 0)

    one = [split(jnp.concatenate([f1_ref[...], -a_ref[...]], 1))]
    two = [split(a_ref[...]), split(f2_ref[...])]
    first = one[0][0].shape[1]
    share_terms(where_ref, 8, [lambda y: f1_rows_ref[y].T], one, 0, other_ref, mine_ref)
    turned = [a_turned, lambda y: f2_rows_ref[y, 0].T]
    share_terms(where_ref, 4, turned, two, first, other_ref, mine_ref)


def level_terms(planes, where_ref, parent_ref, columns_ref, p_rows_ref, f_rows_ref, own_ref, *refs):
    cross_ref, other_ref, mine_ref = refs
    tiles = parent_ref.shape[0] // Y
    count = own_ref.shape[1]

    def left(y):
        return parent_ref[tiles * y : tiles * y + tiles].reshape(352, 176).T

    total = times_columns(planes, where_ref[2], left, columns_ref, count)
    cross_ref[...] = -total
    turned = [lambda y: p_rows_ref[y, 0].T, lambda y: f_rows_ref[y, 0].T]
    factors = [split(total), split(own_ref[...])]
    share_terms(where_ref, planes, turned, factors, 0, other_ref, mine_ref)


def add_pieces(mine_ref, got_ref, *out_refs):
    for step, out_ref in enumerate(out_refs):
        out_ref[...] = mine_ref[step] + got_ref[step]


def finish(*refs):
    in_refs, (*out_refs, turned_ref) = refs[:XS], refs[XS:]
    total = sum(ref[...] for ref in in_refs)
    at = 0
    for out_ref in out_refs:
        run = total[:, at : at + out_ref.shape[1]]
        out_ref[...] = run
        at += out_ref.shape[1]
    turned_ref[...] = run.T


def local(top_factor, panel_two, panel_three, panel_four, factor_two, factor_three, factor_four):
    leaves = lax.axis_size("leaf")
    fronts = lax.axis_size("front")
    share = top_factor.shape[0]
    width = panel_four.shape[1]
    leaf = lax.axis_index("leaf")
    front = lax.axis_index("front")
    z, x, core = leaf // Y, front // CORES, front % CORES
    where = jnp.stack([x, core, z % 8]).astype(jnp.int32)
    y_groups = [list(range(i, i + Y)) for i in range(0, leaves, Y)]

    def from_plane(value, distance):
        pairs = [(i, ((i // Y) ^ distance) * Y + i % Y) for i in range(leaves)]
        return lax.ppermute(value, "leaf", pairs)

    def from_core(value):
        return lax.ppermute(value, "front", [(i, i ^ 1) for i in range(fronts)])

    def shift_x(value, distance):
        pairs = [
            (i, (i // CORES + distance) % XS * CORES + i % CORES) for i in range(fronts)
        ]
        return lax.ppermute(value, "front", pairs)

    def y_gather(value):
        return lax.all_gather(value, "leaf", axis=0, axis_index_groups=y_groups)

    stack = functools.partial(jax.ShapeDtypeStruct, dtype=jnp.float32)
    tile, tiles = stack((share, width)), stack((XS, share, width))
    scalars = pl.BlockSpec(memory_space=pltpu.SMEM)

    def full(value):
        return pl.BlockSpec(value.shape, lambda i: (0,) * len(value.shape))

    def call(kernel, out_shape, in_specs, flops, *args):
        many = isinstance(out_shape, (tuple, list))
        specs = [full(o) for o in (out_shape if many else [out_shape])]
        return pl.pallas_call(
            kernel,
            out_shape=out_shape,
            grid=(1,),
            in_specs=in_specs,
            out_specs=specs if many else specs[0],
            compiler_params=pltpu.CompilerParams(vmem_limit_bytes=VMEM_BYTES),
            cost_estimate=pl.CostEstimate(
                flops=flops, bytes_accessed=8_000_000, transcendentals=0
            ),
        )(*args)

    def front_total(other, mine, widths):
        got = from_core(other)
        piece = stack(mine.shape[1:])
        pieces = call(
            add_pieces, [piece] * XS, [full(mine), full(got)], 1_000_000, mine, got
        )
        parts = [pieces[0]] + [shift_x(pieces[d], d) for d in (1, 3, 2)]
        outs = [stack((share, w)) for w in widths] + [stack((widths[-1], share))]
        return call(finish, outs, [full(piece)] * XS, 1_000_000, *parts)

    def plane_gather(turned, distances):
        turned = turned[None]
        for distance in distances:
            turned = jnp.concatenate([turned, from_plane(turned, distance)], 0)
        gathered = y_gather(turned)
        return gathered.reshape(-1, *gathered.shape[2:])

    def padded(value):
        return jnp.pad(value, ((0, 0), (0, -value.shape[1] % 128)))

    panels = jnp.concatenate([padded(panel_three), padded(panel_two)], 1)
    panels = lax.all_gather(panels, "front", axis=0)

    def columns_spec(lanes, at):
        return pl.BlockSpec((fronts, share, lanes), lambda i: (0, 0, at))

    def rows_spec(at):
        return pl.BlockSpec((Y, 1, share, width), lambda i: (0, at, 0, 0))

    half = share // 2
    first = top_factor.T
    raw = [factor_two, first, from_plane(first, 4)]
    two = call(turn, stack((half, 2 * share)), [full(v) for v in raw], 1_000_000, *raw)
    raw = [two, from_plane(two, 2), panel_three, factor_three]
    near = call(pack, stack((half, 8 * share)), [full(v) for v in raw], 1_000_000, *raw)
    f1, deep, p3 = call(
        join,
        [tile, stack((2, share, width)), tile],
        [scalars, full(near), full(near), pl.BlockSpec(memory_space=pltpu.HBM)],
        1_000_000,
        where,
        near,
        from_plane(near, 1),
        panels,
    )
    rows = y_gather(deep)

    work = 6 * share * share * XS * width
    count = panel_two.shape[1]
    f1_rows = y_gather(f1)
    inner, turned, last = call(
        top_product,
        [stack((share, count)), stack((count, share)), stack((3, share, width))],
        [scalars, full(f1_rows), columns_spec(128, 2)] + [full(tile)] * 3,
        work // 4,
        where,
        f1_rows,
        panels,
        p3,
        panel_four,
        factor_four,
    )
    last_rows = y_gather(last)
    inner_rows = plane_gather(turned, (2, 1))
    widths = [top_factor.shape[1], count, count]
    sums = stack((XS, share, sum(widths)))
    other, mine, p4 = call(
        top_terms,
        [sums, sums, tile],
        [
            scalars,
            full(f1_rows),
            full(top_factor),
            full(inner),
            full(inner_rows),
            rows_spec(0),
            full(factor_two),
            full(tile),
        ],
        work,
        where,
        f1_rows,
        top_factor,
        inner,
        inner_rows,
        rows,
        factor_two,
        panel_four,
    )
    last_panel = lax.all_gather(p4, "front", axis=0)
    *results, turned = front_total(other, mine, widths)

    for planes, factor, distances, sources, specs in (
        (
            2,
            factor_three,
            (2, 1),
            [panels, last_rows, rows],
            [columns_spec(256, 0), rows_spec(0), rows_spec(1)],
        ),
        (
            1,
            factor_four,
            (1,),
            [last_panel, last_rows, last_rows],
            [columns_spec(width, 0), rows_spec(1), rows_spec(2)],
        ),
    ):
        gathered = plane_gather(turned, distances)
        count = factor.shape[1]
        sums = stack((XS, share, count))
        cross, other, mine = call(
            functools.partial(level_terms, planes),
            [stack((share, count)), sums, sums],
            [scalars, full(gathered), *specs, full(factor)],
            4 * work // planes,
            where,
            gathered,
            *sources,
            factor,
        )
        covariance, turned = front_total(other, mine, [count])
        results += [cross, covariance]
    return tuple(results)


def solution(mesh):
    spec = P("front", "leaf")
    return jax.shard_map(
        local, mesh=mesh, in_specs=(spec,) * 7, out_specs=(spec,) * 7, check_vma=False
    )
```

```python
import functools

import jax
import jax.numpy as jnp
from jax import lax
from jax.experimental import pallas as pl
from jax.experimental.pallas import tpu as pltpu
from jax.sharding import PartitionSpec as P

Y = 4
XS = 4
CORES = 2
VMEM_BYTES = 52 * 1024 * 1024


class Staged:

    def __init__(self, source, index, scratch, semaphore):
        self.copy = pltpu.make_async_copy(source.at[index], scratch, semaphore)
        self.scratch, self.waited = scratch, False
        self.copy.start()

    def ready(self):
        if not self.waited:
            self.copy.wait()
            self.waited = True
        return self.scratch


def split(value):
    high = value.astype(jnp.bfloat16)
    low = (value - high.astype(jnp.float32)).astype(jnp.bfloat16)
    return high, low


def product(first, second):
    (fh, fl), (sh, sl) = first, second
    run = functools.partial(jnp.dot, preferred_element_type=jnp.float32)
    return run(fh, sh) + (run(fh, sl) + run(fl, sh))


def block_of(ref, index):
    return ref[:, index * 176 : (index + 1) * 176]


def turn(f2, own, got_ref, out_ref):
    top = jnp.concatenate([own.ready()[...], got_ref[...]], 0)
    out_ref[...] = jnp.concatenate([f2.ready()[...].T, top], 1)


def pack(two_ref, got_ref, p3, f3, out_ref):
    parts = [two_ref[...], got_ref[...]]
    for staged in (p3, f3):
        turned = staged.ready()[...].T
        parts += [turned[:88], turned[88:]]
    out_ref[...] = jnp.concatenate(parts, 1)


def join(where_ref, own_ref, got_ref, panels_ref, f1_ref, rows_ref):
    del panels_ref
    z = where_ref[2]

    def at(which, distance):
        far = ((distance >> 1) & 1) == 1
        own = jnp.where(far, block_of(own_ref, which + 2), block_of(own_ref, which))
        got = jnp.where(far, block_of(got_ref, which + 2), block_of(got_ref, which))
        return jnp.where((distance & 1) == 1, got, own)

    pieces = []
    for plane in range(8):
        distance = plane ^ z
        both = at(1, distance)
        pieces.append(jnp.where((distance >> 2) == 1, both[44:], both[:44]))
    f1_ref[...] = jnp.concatenate(pieces, 0).T
    pieces = [at(0, plane ^ (z % 4)) for plane in range(4)]
    rows_ref[0] = jnp.concatenate(pieces, 0).T
    for which in range(2):
        pieces = []
        for plane in range(2):
            near = plane == (z % 2)
            for index in (4 + 2 * which, 5 + 2 * which):
                pieces.append(
                    jnp.where(near, block_of(own_ref, index), block_of(got_ref, index))
                )
        rows_ref[1 + which] = jnp.concatenate(pieces, 0).T


def share_terms(where_ref, planes, turned, factors, first, other_ref, mine_ref):
    x, core = where_ref[0], where_ref[1]
    last = first + factors[0][0].shape[1]
    for y in range(Y):
        total = None
        for tile, factor in zip(turned, factors):
            term = product(split(tile(y)), factor)
            total = term if total is None else total + term
        width = total.shape[0] // planes
        step = min(width, 176)
        for plane in range(planes):
            for part in range(0, width, step):
                column = (plane * Y + y) * width + part
                block, offset = column // 176, column % 176
                value = total[plane * width + part : plane * width + part + step]
                at = (block // CORES - x) % XS
                same = core == (block % CORES)

                @pl.when(same)
                def _():
                    mine_ref[at, offset : offset + step, first:last] = value

                @pl.when(jnp.logical_not(same))
                def _():
                    other_ref[at, offset : offset + step, first:last] = value


def times_columns(planes, z, left, columns_ref, count):
    total = None
    for y in range(Y):
        if planes == 4:
            parts = [
                columns_ref[p, y * 44 : (y + 1) * 44, :count] for p in range(8)
            ]
        elif planes == 2:
            low = (y % 2) * 88
            parts = []
            for q in range(4):
                p = (z % 4) ^ ((q & 1) * 2 + (q >> 1))
                parts.append(columns_ref[p * 2 + y // 2, low : low + 88, :count])
        else:
            parts = [columns_ref[((z % 2) ^ q) * Y + y, :, :count] for q in range(2)]
        term = product(split(left(y)), split(jnp.concatenate(parts, 0)))
        total = term if total is None else total + term
    return total


def top_product(where_ref, rows_ref, columns, p4_ref, f4_ref, out_ref, turned_ref, last_ref, sems):
    copies = [
        pltpu.make_async_copy(ref, last_ref.at[index], sems.at[index])
        for index, ref in enumerate((p4_ref, f4_ref))
    ]
    for copy in copies:
        copy.start()
    count = out_ref.shape[1]
    left = rows_ref.ready()
    total = times_columns(4, where_ref[2], lambda y: left[y], columns.ready(), count)
    out_ref[...] = total
    turned_ref[...] = total.T
    for copy in copies:
        copy.wait()


def top_terms(where_ref, f1_rows, f1, a_ref, a_rows, f2_rows, f2, other_ref, mine_ref):
    z = where_ref[2]

    def a_turned(y):
        ref = a_rows.ready()
        pieces = []
        for plane in range(4):
            distance = plane ^ (z % 4)
            pieces.append(ref[y * 4 + (distance >> 1) + (distance & 1) * 2])
        return jnp.concatenate(pieces, 0)

    one = [split(jnp.concatenate([f1.ready()[...].T, -a_ref[...]], 1))]
    two = [split(a_ref[...]), split(f2.ready()[...])]
    first = one[0][0].shape[1]
    turned = [lambda y: f1_rows.ready()[y].T]
    share_terms(where_ref, 8, turned, one, 0, other_ref, mine_ref)
    turned = [a_turned, lambda y: f2_rows.ready()[y].T]
    share_terms(where_ref, 4, turned, two, first, other_ref, mine_ref)


def level_terms(planes, where_ref, parent, columns, p_rows, f_rows, own, *refs):
    cross_ref, other_ref, mine_ref = refs
    tiles = parent.scratch.shape[0] // Y
    count = cross_ref.shape[1]

    def left(y):
        return parent.ready()[tiles * y : tiles * y + tiles].reshape(352, 176).T

    total = times_columns(planes, where_ref[2], left, columns.ready(), count)
    cross_ref[...] = -total
    turned = [lambda y: p_rows.ready()[y].T, lambda y: f_rows.ready()[y].T]
    factors = [split(total), split(own.ready()[...])]
    share_terms(where_ref, planes, turned, factors, 0, other_ref, mine_ref)


def add_pieces(mine_ref, got_ref, *out_refs):
    for step, out_ref in enumerate(out_refs):
        out_ref[...] = mine_ref[step] + got_ref[step]


def finish(flip, *refs):
    in_refs, (*out_refs, turned_ref) = refs[:XS], refs[XS:]
    total = sum(ref[...] for ref in in_refs)
    at = 0
    for index, out_ref in enumerate(out_refs):
        turn_it = flip and index == 0
        count = out_ref.shape[0 if turn_it else 1]
        run = total[:, at : at + count]
        out_ref[...] = run.T if turn_it else run
        at += count
    turned_ref[...] = run.T


def local(top_factor, panel_two, panel_three, panel_four, factor_two, factor_three, factor_four):
    leaves = lax.axis_size("leaf")
    fronts = lax.axis_size("front")
    share = top_factor.shape[0]
    width = panel_four.shape[1]
    leaf = lax.axis_index("leaf")
    front = lax.axis_index("front")
    z, x, core = leaf // Y, front // CORES, front % CORES
    where = jnp.stack([x, core, z % 8]).astype(jnp.int32)
    y_groups = [list(range(i, i + Y)) for i in range(0, leaves, Y)]

    def from_plane(value, distance):
        pairs = [(i, ((i // Y) ^ distance) * Y + i % Y) for i in range(leaves)]
        return lax.ppermute(value, "leaf", pairs)

    def from_core(value):
        return lax.ppermute(value, "front", [(i, i ^ 1) for i in range(fronts)])

    def shift_x(value, distance):
        pairs = [
            (i, (i // CORES + distance) % XS * CORES + i % CORES) for i in range(fronts)
        ]
        return lax.ppermute(value, "front", pairs)

    def y_gather(value):
        return lax.all_gather(value, "leaf", axis=0, axis_index_groups=y_groups)

    stack = functools.partial(jax.ShapeDtypeStruct, dtype=jnp.float32)
    tile, tiles = stack((share, width)), stack((XS, share, width))
    def near_by(value):
        return ("near", value)

    def in_hbm(value):
        return ("hbm", value)

    def staged(value, *index):
        index = index or (slice(None),) * value.ndim
        part = jax.eval_shape(lambda v: v[index], value)
        return ("staged", value, index, part)

    def call(kernel, out_shape, flops, *inputs, hbm_outs=(), semaphores=0):
        specs, arrays, scratch = [], [], []
        for kind, value, *rest in inputs:
            arrays.append(value)
            if kind == "near":
                specs.append(pl.BlockSpec(value.shape, lambda i, n=value.ndim: (0,) * n))
            elif kind == "smem":
                specs.append(pl.BlockSpec(memory_space=pltpu.SMEM))
            else:
                specs.append(pl.BlockSpec(memory_space=pltpu.HBM))
            if kind == "staged":
                scratch.append(pltpu.VMEM(rest[1].shape, rest[1].dtype))
        count = len(scratch)
        scratch.append(pltpu.SemaphoreType.DMA((count + 1,)))
        if semaphores:
            scratch.append(pltpu.SemaphoreType.DMA((semaphores,)))

        def body(*refs):
            ins, rest = list(refs[: len(inputs)]), refs[len(inputs) :]
            outs, rest = rest[: len(out_shape)], rest[len(out_shape) :]
            parts, sems, more = rest[:count], rest[count], rest[count + 1 :]
            at = 0
            for index, (kind, *entry) in enumerate(inputs):
                if kind == "staged":
                    ins[index] = Staged(ins[index], entry[1], parts[at], sems.at[at])
                    at += 1
            kernel(*ins, *outs, *more)
            for value in ins:
                if isinstance(value, Staged):
                    value.ready()

        out_specs = [
            pl.BlockSpec(memory_space=pltpu.HBM)
            if index in hbm_outs
            else pl.BlockSpec(o.shape, lambda i, n=len(o.shape): (0,) * n)
            for index, o in enumerate(out_shape)
        ]
        return pl.pallas_call(
            body,
            out_shape=out_shape,
            grid=(1,),
            in_specs=specs,
            out_specs=out_specs,
            scratch_shapes=scratch,
            compiler_params=pltpu.CompilerParams(vmem_limit_bytes=VMEM_BYTES),
            cost_estimate=pl.CostEstimate(
                flops=flops, bytes_accessed=8_000_000, transcendentals=0
            ),
        )(*arrays)

    def front_total(other, mine, widths, flip=False):
        got = from_core(other)
        piece = stack(mine.shape[1:])
        pieces = call(add_pieces, [piece] * XS, 1_000_000, near_by(mine), near_by(got))
        parts = [pieces[0]] + [shift_x(pieces[d], d) for d in (1, 3, 2)]
        outs = [stack((share, w)) for w in widths] + [stack((widths[-1], share))]
        if flip:
            outs[0] = stack(outs[0].shape[::-1])
        kernel = functools.partial(finish, flip)
        return call(kernel, outs, 1_000_000, *[near_by(part) for part in parts])

    def plane_gather(turned, distances):
        turned = turned[None]
        for distance in distances:
            turned = jnp.concatenate([turned, from_plane(turned, distance)], 0)
        gathered = y_gather(turned)
        return gathered.reshape(-1, *gathered.shape[2:])

    def padded(value):
        return jnp.pad(value, ((0, 0), (0, -value.shape[1] % 128)))

    panels = jnp.concatenate([padded(panel_four), padded(panel_two), padded(panel_three)], 1)
    panels = lax.all_gather(panels, "front", axis=0)
    lanes = slice(None), slice(None)
    where = ("smem", where)

    half = share // 2
    first = top_factor.T
    (two,) = call(
        turn,
        [stack((half, 2 * share))],
        1_000_000,
        staged(factor_two),
        staged(first),
        near_by(from_plane(first, 4)),
    )
    (near,) = call(
        pack,
        [stack((half, 8 * share))],
        1_000_000,
        near_by(two),
        near_by(from_plane(two, 2)),
        staged(panel_three),
        staged(factor_three),
    )
    f1, deep = call(
        join,
        [tile, stack((3, share, width))],
        1_000_000,
        where,
        near_by(near),
        near_by(from_plane(near, 1)),
        in_hbm(panels),
    )
    rows = y_gather(deep)

    work = 6 * share * share * XS * width
    count = panel_two.shape[1]
    f1_rows = y_gather(f1)
    inner, turned, last = call(
        top_product,
        [stack((share, count)), stack((count, share)), stack((2, share, width))],
        work // 4,
        where,
        staged(f1_rows),
        staged(panels, *lanes, slice(384, 512)),
        in_hbm(panel_four),
        in_hbm(factor_four),
        hbm_outs=(2,),
        semaphores=2,
    )
    last_rows = y_gather(last)
    inner_rows = plane_gather(turned, (2, 1))
    widths = [top_factor.shape[1], count, count]
    sums = stack((XS, share, sum(widths)))
    other, mine = call(
        top_terms,
        [sums, sums],
        work,
        where,
        staged(f1_rows),
        staged(first),
        near_by(inner),
        staged(inner_rows),
        staged(rows, slice(None), 0),
        staged(factor_two),
    )
    top, *results, turned = front_total(other, mine, widths, flip=True)
    results = [top.T] + results

    for planes, factor, distances, sources, at, columns in (
        (2, factor_three, (2, 1), [rows, rows], (1, 2), slice(512, 768)),
        (1, factor_four, (1,), [last_rows, last_rows], (0, 1), slice(0, 384)),
    ):
        gathered = plane_gather(turned, distances)
        count = factor.shape[1]
        sums = stack((XS, share, count))
        cross, other, mine = call(
            functools.partial(level_terms, planes),
            [stack((share, count)), sums, sums],
            4 * work // planes,
            where,
            staged(gathered),
            staged(panels, *lanes, columns),
            *[staged(source, slice(None), n) for source, n in zip(sources, at)],
            staged(factor),
        )
        covariance, turned = front_total(other, mine, [count])
        results += [cross, covariance]
    return tuple(results)


def solution(mesh):
    spec = P("front", "leaf")
    return jax.shard_map(
        local, mesh=mesh, in_specs=(spec,) * 7, out_specs=(spec,) * 7, check_vma=False
    )
```

```python
import functools

import jax
import jax.numpy as jnp
from jax import lax
from jax.experimental import pallas as pl
from jax.experimental.pallas import tpu as pltpu
from jax.sharding import PartitionSpec as P

Y = 4
XS = 4
CORES = 2
VMEM_BYTES = 52 * 1024 * 1024


class Staged:

    def __init__(self, source, index, scratch, semaphore):
        self.copy = pltpu.make_async_copy(source.at[index], scratch, semaphore)
        self.scratch, self.waited = scratch, False
        self.copy.start()

    def ready(self):
        if not self.waited:
            self.copy.wait()
            self.waited = True
        return self.scratch


def split(value):
    high = value.astype(jnp.bfloat16)
    low = (value - high.astype(jnp.float32)).astype(jnp.bfloat16)
    return high, low


def product(first, second):
    (fh, fl), (sh, sl) = first, second
    run = functools.partial(jnp.dot, preferred_element_type=jnp.float32)
    return run(fh, sh) + (run(fh, sl) + run(fl, sh))


def block_of(ref, index):
    return ref[:, index * 176 : (index + 1) * 176]


def turn(f2, own, got_ref, out_ref):
    top = jnp.concatenate([own.ready()[...], got_ref[...]], 0)
    out_ref[...] = jnp.concatenate([f2.ready()[...].T, top], 1)


def pack(two_ref, got_ref, f3, out_ref):
    turned = f3.ready()[...].T
    parts = [two_ref[...], got_ref[...], turned[:88], turned[88:]]
    out_ref[...] = jnp.concatenate(parts, 1)


def join(where_ref, own_ref, got_ref, panels_ref, f1_ref, rows_ref):
    del panels_ref
    z = where_ref[2]

    def at(which, distance):
        far = ((distance >> 1) & 1) == 1
        own = jnp.where(far, block_of(own_ref, which + 2), block_of(own_ref, which))
        got = jnp.where(far, block_of(got_ref, which + 2), block_of(got_ref, which))
        return jnp.where((distance & 1) == 1, got, own)

    pieces = []
    for plane in range(8):
        distance = plane ^ z
        both = at(1, distance)
        pieces.append(jnp.where((distance >> 2) == 1, both[44:], both[:44]))
    f1_ref[...] = jnp.concatenate(pieces, 0).T
    pieces = [at(0, plane ^ (z % 4)) for plane in range(4)]
    rows_ref[0] = jnp.concatenate(pieces, 0).T
    pieces = []
    for plane in range(2):
        near = plane == (z % 2)
        for index in (4, 5):
            pieces.append(
                jnp.where(near, block_of(own_ref, index), block_of(got_ref, index))
            )
    rows_ref[1] = jnp.concatenate(pieces, 0).T


def sums(planes, turned, factors):
    for y in range(Y):
        total = None
        for tile, factor in zip(turned, factors):
            term = product(split(tile(y)), factor)
            total = term if total is None else total + term
        width = total.shape[0] // planes
        step = min(width, 176)
        for plane in range(planes):
            for part in range(0, width, step):
                column = (plane * Y + y) * width + part
                value = total[plane * width + part : plane * width + part + step]
                yield column // 176, slice(column % 176, column % 176 + step), value


def share_terms(where_ref, planes, turned, factors, other_ref, mine_ref):
    x, core = where_ref[0], where_ref[1]
    for block, rows, value in sums(planes, turned, factors):
        at = (block // CORES - x) % XS
        same = core == (block % CORES)

        @pl.when(same)
        def _():
            mine_ref[at, rows, :] = value

        @pl.when(jnp.logical_not(same))
        def _():
            other_ref[at, rows, :] = value


def times_columns(planes, distances, left, columns_ref, count):
    total = None
    for y in range(Y):
        if planes == 4:
            parts = [
                columns_ref[p, y * 44 : (y + 1) * 44, :count] for p in range(8)
            ]
        elif planes == 2:
            low = (y % 2) * 88
            parts = []
            for q in range(4):
                p = distances ^ ((q & 1) * 2 + (q >> 1)) if distances is not None else q
                parts.append(columns_ref[p * 2 + y // 2, low : low + 88, :count])
        else:
            parts = [columns_ref[(distances ^ q) * Y + y, :, :count] for q in range(2)]
        term = product(split(left(y)), split(jnp.concatenate(parts, 0)))
        total = term if total is None else total + term
    return total


def copied(pairs, sems):
    copies = [
        pltpu.make_async_copy(source, target, sems.at[index])
        for index, (source, target) in enumerate(pairs)
    ]
    for copy in copies:
        copy.start()
    return copies


def top_product(rows, columns, p4_ref, f4_ref, out_ref, turned_ref, last_ref, sems):
    copies = copied([(p4_ref, last_ref.at[0]), (f4_ref, last_ref.at[1])], sems)
    left = rows.ready()
    total = times_columns(4, None, lambda y: left[y], columns.ready(), out_ref.shape[1])
    out_ref[...] = total
    turned_ref[...] = total.T
    for copy in copies:
        copy.wait()


def next_products(where_ref, a_rows, f2_rows, columns, p4_ref, *refs):
    b_ref, g_ref, turned_ref, last_ref, sems = refs
    copies = copied([(p4_ref, last_ref)], sems)
    count, z = b_ref.shape[1], where_ref[2]
    a, f2, right = a_rows.ready(), f2_rows.ready(), columns.ready()
    b = times_columns(2, None, lambda y: f2[y], right, count)
    g = times_columns(
        2, z % 4, lambda y: a[4 * y : 4 * y + 4].reshape(352, 176).T, right, count
    )
    b_ref[...], g_ref[...] = b, g
    turned_ref[0], turned_ref[1] = b.T, g.T
    for copy in copies:
        copy.wait()


def pieces_of(ref, y, planes, z):
    pieces = []
    for plane in range(planes):
        distance = plane ^ (z % planes)
        at = distance if planes == 2 else (distance >> 1) + (distance & 1) * 2
        pieces.append(ref[y * planes + at])
    return jnp.concatenate(pieces, 0)


def third_terms(where_ref, b_ref, g_ref, b_rows, g_rows, f3_rows, f3, other_ref, mine_ref):
    z = where_ref[2]
    turned = [
        lambda y: pieces_of(b_rows.ready(), y, 2, z),
        lambda y: pieces_of(g_rows.ready(), y, 2, z),
        lambda y: f3_rows.ready()[y].T,
    ]
    factors = [split(b_ref[...]), split(g_ref[...]), split(f3.ready()[...])]
    share_terms(where_ref, 2, turned, factors, other_ref, mine_ref)


def early_terms(where_ref, f1_rows, f1, a, a_rows, f2_rows, f2, b, g, arrived_ref, out_ref):
    del arrived_ref
    z, inner = where_ref[2], a.ready()[...]
    factors = [split(jnp.concatenate([f1.ready()[...].T, -inner], 1))]
    first = factors[0][0].shape[1]
    for block, rows, value in sums(8, [lambda y: f1_rows.ready()[y].T], factors):
        out_ref[block, rows, :first] = value
    turned = [
        lambda y: pieces_of(a_rows.ready(), y, 4, z),
        lambda y: f2_rows.ready()[y].T,
    ]
    factors = [
        split(jnp.concatenate([inner, -g.ready()[...]], 1)),
        split(jnp.concatenate([f2.ready()[...], -b.ready()[...]], 1)),
    ]
    for block, rows, value in sums(4, turned, factors):
        out_ref[block, rows, first:] = value


def last_terms(where_ref, parent, columns, p_rows, f_rows, own, *refs):
    cross_ref, other_ref, mine_ref = refs
    count = cross_ref.shape[1]

    def left(y):
        return parent.ready()[2 * y : 2 * y + 2].reshape(352, 176).T

    total = times_columns(1, where_ref[2] % 2, left, columns.ready(), count)
    cross_ref[...] = -total
    turned = [lambda y: p_rows.ready()[y].T, lambda y: f_rows.ready()[y].T]
    factors = [split(total), split(own.ready()[...])]
    share_terms(where_ref, 1, turned, factors, other_ref, mine_ref)


def add_pieces(mine, got_ref, *out_refs):
    mine_ref = mine.ready()
    for step, out_ref in enumerate(out_refs):
        out_ref[...] = mine_ref[step] + got_ref[step]


def finish(*refs):
    *in_refs, out_ref, turned_ref = refs
    total = sum(ref[...] for ref in in_refs)
    out_ref[...] = total
    turned_ref[...] = total.T


def local(top_factor, panel_two, panel_three, panel_four, factor_two, factor_three, factor_four):
    leaves = lax.axis_size("leaf")
    fronts = lax.axis_size("front")
    share = top_factor.shape[0]
    width = panel_four.shape[1]
    leaf = lax.axis_index("leaf")
    front = lax.axis_index("front")
    z, x, core = leaf // Y, front // CORES, front % CORES
    where = jnp.stack([x, core, z % 8]).astype(jnp.int32)
    y_groups = [list(range(i, i + Y)) for i in range(0, leaves, Y)]

    def from_plane(value, distance):
        pairs = [(i, ((i // Y) ^ distance) * Y + i % Y) for i in range(leaves)]
        return lax.ppermute(value, "leaf", pairs)

    def from_core(value):
        return lax.ppermute(value, "front", [(i, i ^ 1) for i in range(fronts)])

    def shift_x(value, distance):
        pairs = [
            (i, (i // CORES + distance) % XS * CORES + i % CORES) for i in range(fronts)
        ]
        return lax.ppermute(value, "front", pairs)

    def y_gather(value):
        return lax.all_gather(value, "leaf", axis=0, axis_index_groups=y_groups)

    stack = functools.partial(jax.ShapeDtypeStruct, dtype=jnp.float32)
    tile, tiles = stack((share, width)), stack((XS, share, width))
    def near_by(value):
        return ("near", value)

    def in_hbm(value):
        return ("hbm", value)

    def staged(value, *index):
        index = index or (slice(None),) * value.ndim
        part = jax.eval_shape(lambda v: v[index], value)
        return ("staged", value, index, part)

    def call(kernel, out_shape, flops, *inputs, hbm_outs=(), semaphores=0):
        specs, arrays, scratch = [], [], []
        for kind, value, *rest in inputs:
            arrays.append(value)
            if kind == "near":
                specs.append(pl.BlockSpec(value.shape, lambda i, n=value.ndim: (0,) * n))
            elif kind == "smem":
                specs.append(pl.BlockSpec(memory_space=pltpu.SMEM))
            else:
                specs.append(pl.BlockSpec(memory_space=pltpu.HBM))
            if kind == "staged":
                scratch.append(pltpu.VMEM(rest[1].shape, rest[1].dtype))
        count = len(scratch)
        scratch.append(pltpu.SemaphoreType.DMA((count + 1,)))
        if semaphores:
            scratch.append(pltpu.SemaphoreType.DMA((semaphores,)))

        def body(*refs):
            ins, rest = list(refs[: len(inputs)]), refs[len(inputs) :]
            outs, rest = rest[: len(out_shape)], rest[len(out_shape) :]
            parts, sems, more = rest[:count], rest[count], rest[count + 1 :]
            at = 0
            for index, (kind, *entry) in enumerate(inputs):
                if kind == "staged":
                    ins[index] = Staged(ins[index], entry[1], parts[at], sems.at[at])
                    at += 1
            kernel(*ins, *outs, *more)
            for value in ins:
                if isinstance(value, Staged):
                    value.ready()

        out_specs = [
            pl.BlockSpec(memory_space=pltpu.HBM)
            if index in hbm_outs
            else pl.BlockSpec(o.shape, lambda i, n=len(o.shape): (0,) * n)
            for index, o in enumerate(out_shape)
        ]
        return pl.pallas_call(
            body,
            out_shape=out_shape,
            grid=(1,),
            in_specs=specs,
            out_specs=out_specs,
            scratch_shapes=scratch,
            compiler_params=pltpu.CompilerParams(vmem_limit_bytes=VMEM_BYTES),
            cost_estimate=pl.CostEstimate(
                flops=flops, bytes_accessed=8_000_000, transcendentals=0
            ),
        )(*arrays)

    def front_total(other, mine):
        got = from_core(other)
        piece = stack(mine.shape[1:])
        pieces = call(add_pieces, [piece] * XS, 1_000_000, staged(mine), near_by(got))
        parts = [pieces[0]] + [shift_x(pieces[d], d) for d in (1, 3, 2)]
        outs = [piece, stack(piece.shape[::-1])]
        outs = call(finish, outs, 1_000_000, *[near_by(part) for part in parts])
        return *outs, parts[1]

    def plane_gather(parts):
        gathered = y_gather(jnp.stack(parts))
        return gathered.reshape(-1, *gathered.shape[2:])

    def padded(value):
        return jnp.pad(value, ((0, 0), (0, -value.shape[1] % 128)))

    panels = jnp.concatenate([padded(panel_three), padded(panel_two)], 1)
    panels = lax.all_gather(panels, "front", axis=0)
    lanes = slice(None), slice(None)
    where = ("smem", where)

    half = share // 2
    first = top_factor.T
    (two,) = call(
        turn,
        [stack((half, 2 * share))],
        1_000_000,
        staged(factor_two),
        staged(first),
        near_by(from_plane(first, 4)),
    )
    (near,) = call(
        pack,
        [stack((half, 6 * share))],
        1_000_000,
        near_by(two),
        near_by(from_plane(two, 2)),
        staged(factor_three),
    )
    f1, deep = call(
        join,
        [tile, stack((2, share, width))],
        1_000_000,
        where,
        near_by(near),
        near_by(from_plane(near, 1)),
        in_hbm(panels),
    )
    rows = y_gather(deep)
    f1_rows = y_gather(f1)

    work = 6 * share * share * XS * width
    count = panel_two.shape[1]
    inner, turned, last = call(
        top_product,
        [stack((share, count)), stack((count, share)), stack((2, share, width))],
        work // 4,
        staged(f1_rows),
        staged(panels, *lanes, slice(256, 384)),
        in_hbm(panel_four),
        in_hbm(factor_four),
        hbm_outs=(2,),
        semaphores=2,
    )
    last_rows = y_gather(last)
    a_rows = plane_gather([turned] + [from_plane(turned, d) for d in (2, 1, 3)])
    b, g, turned, p4 = call(
        next_products,
        [stack((share, share))] * 2 + [stack((2, share, share)), tile],
        work,
        where,
        staged(a_rows),
        staged(rows, slice(None), 0),
        staged(panels, *lanes, slice(0, 256)),
        in_hbm(panel_four),
        hbm_outs=(3,),
        semaphores=1,
    )
    last_panel = lax.all_gather(p4, "front", axis=0)
    got = from_plane(turned, 1)
    b_rows, g_rows = (plane_gather([turned[i], got[i]]) for i in range(2))

    half_sums = stack((XS, share, share))
    other, mine = call(
        third_terms,
        [half_sums, half_sums],
        2 * work,
        where,
        near_by(b),
        near_by(g),
        staged(b_rows),
        staged(g_rows),
        staged(rows, slice(None), 1),
        staged(factor_three),
    )
    cov_three, turned, arrived = front_total(other, mine)

    widths = [top_factor.shape[1], count, count, share]
    (early,) = call(
        early_terms,
        [stack((fronts, share, sum(widths)))],
        2 * work,
        where,
        staged(f1_rows),
        staged(first),
        staged(inner),
        staged(a_rows),
        staged(rows, slice(None), 0),
        staged(factor_two),
        staged(b),
        staged(g),
        near_by(arrived),
    )
    early = early.reshape(fronts * share, -1)
    early = lax.psum_scatter(early, "front", scatter_dimension=0, tiled=True)
    at = [sum(widths[:i]) for i in range(len(widths))]
    cov_one, cross_two, cov_two, cross_three = (
        early[:, i : i + w] for i, w in zip(at, widths)
    )

    parent_rows = plane_gather([turned, from_plane(turned, 1)])
    cross_four, other, mine = call(
        last_terms,
        [tile, tiles, tiles],
        4 * work,
        where,
        staged(parent_rows),
        staged(last_panel),
        staged(last_rows, slice(None), 0),
        staged(last_rows, slice(None), 1),
        staged(factor_four),
    )
    cov_four, *_ = front_total(other, mine)
    return cov_one, cross_two, cov_two, cross_three, cov_three, cross_four, cov_four


def solution(mesh):
    spec = P("front", "leaf")
    return jax.shard_map(
        local, mesh=mesh, in_specs=(spec,) * 7, out_specs=(spec,) * 7, check_vma=False
    )
```

```python
import functools

import jax
import jax.numpy as jnp
from jax import lax
from jax.experimental import pallas as pl
from jax.experimental.pallas import tpu as pltpu
from jax.sharding import PartitionSpec as P

Y = 4
XS = 4
CORES = 2
VMEM_BYTES = 52 * 1024 * 1024


class Staged:

    def __init__(self, source, index, scratch, semaphore):
        self.copy = pltpu.make_async_copy(source.at[index], scratch, semaphore)
        self.scratch, self.waited = scratch, False
        self.copy.start()

    def ready(self):
        if not self.waited:
            self.copy.wait()
            self.waited = True
        return self.scratch


def split(value):
    high = value.astype(jnp.bfloat16)
    low = (value - high.astype(jnp.float32)).astype(jnp.bfloat16)
    return high, low


def product(first, second):
    (fh, fl), (sh, sl) = first, second
    run = functools.partial(jnp.dot, preferred_element_type=jnp.float32)
    return run(fh, sh) + (run(fh, sl) + run(fl, sh))


def block_of(ref, index):
    return ref[:, index * 176 : (index + 1) * 176]


def turn(f2, own, got_ref, out_ref):
    top = jnp.concatenate([own.ready()[...], got_ref[...]], 0)
    out_ref[...] = jnp.concatenate([f2.ready()[...].T, top], 1)


def pack(two_ref, got_ref, f3, out_ref):
    turned = f3.ready()[...].T
    parts = [two_ref[...], got_ref[...], turned[:88], turned[88:]]
    out_ref[...] = jnp.concatenate(parts, 1)


def join(where_ref, own_ref, got_ref, panels_ref, f1_ref, rows_ref):
    del panels_ref
    z = where_ref[2]

    def at(which, distance):
        far = ((distance >> 1) & 1) == 1
        own = jnp.where(far, block_of(own_ref, which + 2), block_of(own_ref, which))
        got = jnp.where(far, block_of(got_ref, which + 2), block_of(got_ref, which))
        return jnp.where((distance & 1) == 1, got, own)

    pieces = []
    for plane in range(8):
        distance = plane ^ z
        both = at(1, distance)
        pieces.append(jnp.where((distance >> 2) == 1, both[44:], both[:44]))
    f1_ref[...] = jnp.concatenate(pieces, 0).T
    pieces = [at(0, plane ^ (z % 4)) for plane in range(4)]
    rows_ref[0] = jnp.concatenate(pieces, 0).T
    pieces = []
    for plane in range(2):
        near = plane == (z % 2)
        for index in (4, 5):
            pieces.append(
                jnp.where(near, block_of(own_ref, index), block_of(got_ref, index))
            )
    rows_ref[1] = jnp.concatenate(pieces, 0).T


def sums(planes, turned, factors):
    for y in range(Y):
        total = None
        for tile, factor in zip(turned, factors):
            term = product(split(tile(y)), factor)
            total = term if total is None else total + term
        width = total.shape[0] // planes
        step = min(width, 176)
        for plane in range(planes):
            for part in range(0, width, step):
                column = (plane * Y + y) * width + part
                value = total[plane * width + part : plane * width + part + step]
                yield column // 176, slice(column % 176, column % 176 + step), value


def share_terms(where_ref, planes, turned, factors, other_ref, mine_ref):
    x, core = where_ref[0], where_ref[1]
    for block, rows, value in sums(planes, turned, factors):
        at = (block // CORES - x) % XS
        same = core == (block % CORES)

        @pl.when(same)
        def _():
            mine_ref[at, rows, :] = value

        @pl.when(jnp.logical_not(same))
        def _():
            other_ref[at, rows, :] = value


def times_columns(planes, distances, left, columns_ref, count):
    total = None
    for y in range(Y):
        if planes == 4:
            parts = [
                columns_ref[p, y * 44 : (y + 1) * 44, :count] for p in range(8)
            ]
        elif planes == 2:
            low = (y % 2) * 88
            parts = []
            for q in range(4):
                p = distances ^ ((q & 1) * 2 + (q >> 1)) if distances is not None else q
                parts.append(columns_ref[p * 2 + y // 2, low : low + 88, :count])
        else:
            parts = [columns_ref[(distances ^ q) * Y + y, :, :count] for q in range(2)]
        term = product(split(left(y)), split(jnp.concatenate(parts, 0)))
        total = term if total is None else total + term
    return total


def copied(pairs, sems):
    copies = [
        pltpu.make_async_copy(source, target, sems.at[index])
        for index, (source, target) in enumerate(pairs)
    ]
    for copy in copies:
        copy.start()
    return copies


def top_product(rows, columns, p4_ref, out_ref, turned_ref, last_ref, sems):
    copies = copied([(p4_ref, last_ref)], sems)
    left = rows.ready()
    total = times_columns(4, None, lambda y: left[y], columns.ready(), out_ref.shape[1])
    out_ref[...] = total
    turned_ref[...] = total.T
    for copy in copies:
        copy.wait()


def next_products(where_ref, a_rows, f2_rows, columns, b_ref, g_ref, turned_ref):
    count, z = b_ref.shape[1], where_ref[2]
    a, f2, right = a_rows.ready(), f2_rows.ready(), columns.ready()
    b = times_columns(2, None, lambda y: f2[y], right, count)
    g = times_columns(
        2, z % 4, lambda y: a[4 * y : 4 * y + 4].reshape(352, 176).T, right, count
    )
    b_ref[...], g_ref[...] = b, g
    turned_ref[0], turned_ref[1] = b.T, g.T


def pieces_of(ref, y, planes, z):
    pieces = []
    for plane in range(planes):
        distance = plane ^ (z % planes)
        at = distance if planes == 2 else (distance >> 1) + (distance & 1) * 2
        pieces.append(ref[y * planes + at])
    return jnp.concatenate(pieces, 0)


def third_terms(where_ref, b_ref, g_ref, b_rows, g_rows, f3_rows, f3, p4_ref, f4_ref, *refs):
    other_ref, mine_ref, last_ref, sems = refs
    copies = copied([(p4_ref, last_ref.at[0]), (f4_ref, last_ref.at[1])], sems)
    z = where_ref[2]
    turned = [
        lambda y: pieces_of(b_rows.ready(), y, 2, z),
        lambda y: pieces_of(g_rows.ready(), y, 2, z),
        lambda y: f3_rows.ready()[y].T,
    ]
    factors = [split(b_ref[...]), split(g_ref[...]), split(f3.ready()[...])]
    share_terms(where_ref, 2, turned, factors, other_ref, mine_ref)
    for copy in copies:
        copy.wait()


def early_terms(where_ref, f1_rows, f1, a, a_rows, f2_rows, f2, b, g, out_ref):
    z, inner = where_ref[2], a.ready()[...]
    factors = [split(jnp.concatenate([f1.ready()[...].T, -inner], 1))]
    first = factors[0][0].shape[1]
    for block, rows, value in sums(8, [lambda y: f1_rows.ready()[y].T], factors):
        out_ref[block, rows, :first] = value
    turned = [
        lambda y: pieces_of(a_rows.ready(), y, 4, z),
        lambda y: f2_rows.ready()[y].T,
    ]
    factors = [
        split(jnp.concatenate([inner, -g.ready()[...]], 1)),
        split(jnp.concatenate([f2.ready()[...], -b.ready()[...]], 1)),
    ]
    for block, rows, value in sums(4, turned, factors):
        out_ref[block, rows, first:] = value


def cut(early_ref, turned_ref, *out_refs):
    first, at = turned_ref.shape[0], turned_ref.shape[0]
    turned_ref[...] = early_ref[:, :first].T
    for out_ref in out_refs:
        out_ref[...] = early_ref[:, at : at + out_ref.shape[1]]
        at += out_ref.shape[1]


def last_terms(where_ref, parent, columns, p_rows, f_rows, own, *refs):
    cross_ref, other_ref, mine_ref = refs
    count = cross_ref.shape[1]

    def left(y):
        return parent.ready()[2 * y : 2 * y + 2].reshape(352, 176).T

    total = times_columns(1, where_ref[2] % 2, left, columns.ready(), count)
    cross_ref[...] = -total
    turned = [lambda y: p_rows.ready()[y].T, lambda y: f_rows.ready()[y].T]
    factors = [split(total), split(own.ready()[...])]
    share_terms(where_ref, 1, turned, factors, other_ref, mine_ref)


def add_pieces(mine, got_ref, *out_refs):
    mine_ref = mine.ready()
    for step, out_ref in enumerate(out_refs):
        out_ref[...] = mine_ref[step] + got_ref[step]


def finish(*refs):
    *in_refs, out_ref, turned_ref = refs
    total = sum(ref[...] for ref in in_refs)
    out_ref[...] = total
    turned_ref[...] = total.T


def local(top_factor, panel_two, panel_three, panel_four, factor_two, factor_three, factor_four):
    leaves = lax.axis_size("leaf")
    fronts = lax.axis_size("front")
    share = top_factor.shape[0]
    width = panel_four.shape[1]
    leaf = lax.axis_index("leaf")
    front = lax.axis_index("front")
    z, x, core = leaf // Y, front // CORES, front % CORES
    where = jnp.stack([x, core, z % 8]).astype(jnp.int32)
    y_groups = [list(range(i, i + Y)) for i in range(0, leaves, Y)]

    def from_plane(value, distance):
        pairs = [(i, ((i // Y) ^ distance) * Y + i % Y) for i in range(leaves)]
        return lax.ppermute(value, "leaf", pairs)

    def from_core(value):
        return lax.ppermute(value, "front", [(i, i ^ 1) for i in range(fronts)])

    def shift_x(value, distance):
        pairs = [
            (i, (i // CORES + distance) % XS * CORES + i % CORES) for i in range(fronts)
        ]
        return lax.ppermute(value, "front", pairs)

    def y_gather(value):
        return lax.all_gather(value, "leaf", axis=0, axis_index_groups=y_groups)

    stack = functools.partial(jax.ShapeDtypeStruct, dtype=jnp.float32)
    tile, tiles = stack((share, width)), stack((XS, share, width))
    def near_by(value):
        return ("near", value)

    def in_hbm(value):
        return ("hbm", value)

    def staged(value, *index):
        index = index or (slice(None),) * value.ndim
        part = jax.eval_shape(lambda v: v[index], value)
        return ("staged", value, index, part)

    def call(kernel, out_shape, flops, *inputs, hbm_outs=(), semaphores=0):
        specs, arrays, scratch = [], [], []
        for kind, value, *rest in inputs:
            arrays.append(value)
            if kind == "near":
                specs.append(pl.BlockSpec(value.shape, lambda i, n=value.ndim: (0,) * n))
            elif kind == "smem":
                specs.append(pl.BlockSpec(memory_space=pltpu.SMEM))
            else:
                specs.append(pl.BlockSpec(memory_space=pltpu.HBM))
            if kind == "staged":
                scratch.append(pltpu.VMEM(rest[1].shape, rest[1].dtype))
        count = len(scratch)
        scratch.append(pltpu.SemaphoreType.DMA((count + 1,)))
        if semaphores:
            scratch.append(pltpu.SemaphoreType.DMA((semaphores,)))

        def body(*refs):
            ins, rest = list(refs[: len(inputs)]), refs[len(inputs) :]
            outs, rest = rest[: len(out_shape)], rest[len(out_shape) :]
            parts, sems, more = rest[:count], rest[count], rest[count + 1 :]
            at = 0
            for index, (kind, *entry) in enumerate(inputs):
                if kind == "staged":
                    ins[index] = Staged(ins[index], entry[1], parts[at], sems.at[at])
                    at += 1
            kernel(*ins, *outs, *more)
            for value in ins:
                if isinstance(value, Staged):
                    value.ready()

        out_specs = [
            pl.BlockSpec(memory_space=pltpu.HBM)
            if index in hbm_outs
            else pl.BlockSpec(o.shape, lambda i, n=len(o.shape): (0,) * n)
            for index, o in enumerate(out_shape)
        ]
        return pl.pallas_call(
            body,
            out_shape=out_shape,
            grid=(1,),
            in_specs=specs,
            out_specs=out_specs,
            scratch_shapes=scratch,
            compiler_params=pltpu.CompilerParams(vmem_limit_bytes=VMEM_BYTES),
            cost_estimate=pl.CostEstimate(
                flops=flops, bytes_accessed=8_000_000, transcendentals=0
            ),
        )(*arrays)

    def front_total(other, mine):
        got = from_core(other)
        piece = stack(mine.shape[1:])
        pieces = call(add_pieces, [piece] * XS, 1_000_000, staged(mine), near_by(got))
        parts = [pieces[0]] + [shift_x(pieces[d], d) for d in (1, 3, 2)]
        outs = [piece, stack(piece.shape[::-1])]
        outs = call(finish, outs, 1_000_000, *[near_by(part) for part in parts])
        return outs

    def plane_gather(parts):
        gathered = y_gather(jnp.stack(parts))
        return gathered.reshape(-1, *gathered.shape[2:])

    def padded(value):
        return jnp.pad(value, ((0, 0), (0, -value.shape[1] % 128)))

    panels = jnp.concatenate([padded(panel_three), padded(panel_two)], 1)
    panels = lax.all_gather(panels, "front", axis=0)
    lanes = slice(None), slice(None)
    where = ("smem", where)

    half = share // 2
    first = top_factor.T
    (two,) = call(
        turn,
        [stack((half, 2 * share))],
        1_000_000,
        staged(factor_two),
        staged(first),
        near_by(from_plane(first, 4)),
    )
    (near,) = call(
        pack,
        [stack((half, 6 * share))],
        1_000_000,
        near_by(two),
        near_by(from_plane(two, 2)),
        staged(factor_three),
    )
    f1, deep = call(
        join,
        [tile, stack((2, share, width))],
        1_000_000,
        where,
        near_by(near),
        near_by(from_plane(near, 1)),
        in_hbm(panels),
    )
    rows = y_gather(deep)
    f1_rows = y_gather(f1)

    work = 6 * share * share * XS * width
    count = panel_two.shape[1]
    inner, turned, p4 = call(
        top_product,
        [stack((share, count)), stack((count, share)), tile],
        work // 4,
        staged(f1_rows),
        staged(panels, *lanes, slice(256, 384)),
        in_hbm(panel_four),
        hbm_outs=(2,),
        semaphores=1,
    )
    last_panel = lax.all_gather(p4, "front", axis=0)
    a_rows = plane_gather([turned] + [from_plane(turned, d) for d in (2, 1, 3)])
    b, g, turned = call(
        next_products,
        [stack((share, share))] * 2 + [stack((2, share, share))],
        work,
        where,
        staged(a_rows),
        staged(rows, slice(None), 0),
        staged(panels, *lanes, slice(0, 256)),
    )
    got = from_plane(turned, 1)
    b_rows, g_rows = (plane_gather([turned[i], got[i]]) for i in range(2))

    half_sums = stack((XS, share, share))
    other, mine, last = call(
        third_terms,
        [half_sums, half_sums, stack((2, share, width))],
        2 * work,
        where,
        near_by(b),
        near_by(g),
        staged(b_rows),
        staged(g_rows),
        staged(rows, slice(None), 1),
        staged(factor_three),
        in_hbm(panel_four),
        in_hbm(factor_four),
        hbm_outs=(2,),
        semaphores=2,
    )
    last_rows = y_gather(last)
    cov_three, turned = front_total(other, mine)

    widths = [top_factor.shape[1], count, count, share]
    (early,) = call(
        early_terms,
        [stack((fronts, share, sum(widths)))],
        2 * work,
        where,
        staged(f1_rows),
        staged(first),
        staged(inner),
        staged(a_rows),
        staged(rows, slice(None), 0),
        staged(factor_two),
        staged(b),
        staged(g),
    )
    early, turned = lax.optimization_barrier((early, turned))
    early = early.reshape(fronts * share, -1)
    early = lax.psum_scatter(early, "front", scatter_dimension=0, tiled=True)
    cuts = [stack((widths[0], share))] + [stack((share, w)) for w in widths[1:]]
    cov_one, cross_two, cov_two, cross_three = call(cut, cuts, 1_000_000, near_by(early))

    parent_rows = plane_gather([turned, from_plane(turned, 1)])
    cross_four, other, mine = call(
        last_terms,
        [tile, tiles, tiles],
        4 * work,
        where,
        staged(parent_rows),
        staged(last_panel),
        staged(last_rows, slice(None), 0),
        staged(last_rows, slice(None), 1),
        staged(factor_four),
    )
    cov_four, _ = front_total(other, mine)
    return cov_one.T, cross_two, cov_two, cross_three, cov_three, cross_four, cov_four


def solution(mesh):
    spec = P("front", "leaf")
    return jax.shard_map(
        local, mesh=mesh, in_specs=(spec,) * 7, out_specs=(spec,) * 7, check_vma=False
    )
```

```python
import functools

import jax
import jax.numpy as jnp
from jax import lax
from jax.experimental import pallas as pl
from jax.experimental.pallas import tpu as pltpu
from jax.sharding import PartitionSpec as P

Y = 4
XS = 4
CORES = 2
VMEM_BYTES = 52 * 1024 * 1024


class Staged:

    def __init__(self, source, index, scratch, semaphore):
        self.copy = pltpu.make_async_copy(source.at[index], scratch, semaphore)
        self.scratch, self.waited = scratch, False
        self.copy.start()

    def ready(self):
        if not self.waited:
            self.copy.wait()
            self.waited = True
        return self.scratch


def split(value):
    high = value.astype(jnp.bfloat16)
    low = (value - high.astype(jnp.float32)).astype(jnp.bfloat16)
    return high, low


def product(first, second):
    (fh, fl), (sh, sl) = first, second
    run = functools.partial(jnp.dot, preferred_element_type=jnp.float32)
    return run(fh, sh) + (run(fh, sl) + run(fl, sh))


def block_of(ref, index):
    return ref[:, index * 176 : (index + 1) * 176]


def turn(f2, own, got_ref, out_ref):
    top = jnp.concatenate([own.ready()[...], got_ref[...]], 0)
    out_ref[...] = jnp.concatenate([f2.ready()[...].T, top], 1)


def pack(two_ref, got_ref, f3, out_ref):
    turned = f3.ready()[...].T
    parts = [two_ref[...], got_ref[...], turned[:88], turned[88:]]
    out_ref[...] = jnp.concatenate(parts, 1)


def join(where_ref, own_ref, got_ref, panels_ref, f1_ref, rows_ref):
    del panels_ref
    z = where_ref[2]

    def at(which, distance):
        far = ((distance >> 1) & 1) == 1
        own = jnp.where(far, block_of(own_ref, which + 2), block_of(own_ref, which))
        got = jnp.where(far, block_of(got_ref, which + 2), block_of(got_ref, which))
        return jnp.where((distance & 1) == 1, got, own)

    pieces = []
    for plane in range(8):
        distance = plane ^ z
        both = at(1, distance)
        pieces.append(jnp.where((distance >> 2) == 1, both[44:], both[:44]))
    f1_ref[...] = jnp.concatenate(pieces, 0).T
    pieces = [at(0, plane ^ (z % 4)) for plane in range(4)]
    rows_ref[0] = jnp.concatenate(pieces, 0).T
    pieces = []
    for plane in range(2):
        near = plane == (z % 2)
        for index in (4, 5):
            pieces.append(
                jnp.where(near, block_of(own_ref, index), block_of(got_ref, index))
            )
    rows_ref[1] = jnp.concatenate(pieces, 0).T


def sums(planes, turned, factors):
    for y in range(Y):
        total = None
        for tile, factor in zip(turned, factors):
            term = product(split(tile(y)), factor)
            total = term if total is None else total + term
        width = total.shape[0] // planes
        step = min(width, 176)
        for plane in range(planes):
            for part in range(0, width, step):
                column = (plane * Y + y) * width + part
                value = total[plane * width + part : plane * width + part + step]
                yield column // 176, slice(column % 176, column % 176 + step), value


def times_columns(planes, distances, left, columns_ref, count):
    total = None
    for y in range(Y):
        if planes == 4:
            parts = [
                columns_ref[p, y * 44 : (y + 1) * 44, :count] for p in range(8)
            ]
        elif planes == 2:
            low = (y % 2) * 88
            parts = []
            for q in range(4):
                p = distances ^ ((q & 1) * 2 + (q >> 1)) if distances is not None else q
                parts.append(columns_ref[p * 2 + y // 2, low : low + 88, :count])
        else:
            parts = [columns_ref[(distances ^ q) * Y + y, :, :count] for q in range(2)]
        term = product(split(left(y)), split(jnp.concatenate(parts, 0)))
        total = term if total is None else total + term
    return total


def top_product(rows, columns, out_ref, turned_ref):
    left = rows.ready()
    total = times_columns(4, None, lambda y: left[y], columns.ready(), out_ref.shape[1])
    out_ref[...] = total
    turned_ref[...] = total.T


def next_products(where_ref, a_rows, f2_rows, columns, b_ref, g_ref, turned_ref):
    count, z = b_ref.shape[1], where_ref[2]
    a, f2, right = a_rows.ready(), f2_rows.ready(), columns.ready()
    b = times_columns(2, None, lambda y: f2[y], right, count)
    g = times_columns(
        2, z % 4, lambda y: a[4 * y : 4 * y + 4].reshape(352, 176).T, right, count
    )
    b_ref[...], g_ref[...] = b, g
    turned_ref[0], turned_ref[1] = b.T, g.T


def pieces_of(ref, y, planes, z):
    pieces = []
    for plane in range(planes):
        distance = plane ^ (z % planes)
        at = distance if planes == 2 else (distance >> 1) + (distance & 1) * 2
        pieces.append(ref[y * planes + at])
    return jnp.concatenate(pieces, 0)


def third_terms(flip, where_ref, b_ref, g_ref, b_rows, g_rows, f3_rows, f3, out_ref):
    x, half, z = where_ref[0], where_ref[1] ^ flip, where_ref[2]
    factors = [split(b_ref[...]), split(g_ref[...]), split(f3.ready()[...])]
    for i in range(2):
        y = 2 * i + half
        turned = [
            pieces_of(b_rows.ready(), y, 2, z),
            pieces_of(g_rows.ready(), y, 2, z),
            f3_rows.ready()[y].T,
        ]
        total = sum(product(split(t), factor) for t, factor in zip(turned, factors))
        for plane in range(2):
            out_ref[(plane * 2 + i - x) % XS] = total[plane * 176 : plane * 176 + 176]


def early_terms(where_ref, f1_rows, f1, a, a_rows, f2_rows, f2, b, g, out_ref):
    z, inner = where_ref[2], a.ready()[...]
    factors = [split(jnp.concatenate([f1.ready()[...].T, -inner], 1))]
    first = factors[0][0].shape[1]
    for block, rows, value in sums(8, [lambda y: f1_rows.ready()[y].T], factors):
        out_ref[block, rows, :first] = value
    turned = [
        lambda y: pieces_of(a_rows.ready(), y, 4, z),
        lambda y: f2_rows.ready()[y].T,
    ]
    factors = [
        split(jnp.concatenate([inner, -g.ready()[...]], 1)),
        split(jnp.concatenate([f2.ready()[...], -b.ready()[...]], 1)),
    ]
    for block, rows, value in sums(4, turned, factors):
        out_ref[block, rows, first:] = value


def cut(early_ref, turned_ref, *out_refs):
    first, at = turned_ref.shape[0], turned_ref.shape[0]
    turned_ref[...] = early_ref[:, :first].T
    for out_ref in out_refs:
        out_ref[...] = early_ref[:, at : at + out_ref.shape[1]]
        at += out_ref.shape[1]


def last_half(flip, where_ref, p_rows, f_rows, factors, out_ref):
    x, half = where_ref[0], where_ref[1] ^ flip
    for y in range(Y):
        total = 0.0
        for rows, factor in zip((p_rows, f_rows), factors):
            tile = rows.ready()[y]
            tile = jnp.where(half == 0, tile[:, :176], tile[:, 176:])
            total += product(split(tile.T), factor)
        out_ref[(y - x) % XS] = total


def last_other(where_ref, parent, columns, p_rows, f_rows, own, cross_ref, other_ref):
    def left(y):
        return parent.ready()[2 * y : 2 * y + 2].reshape(352, 176).T

    count = cross_ref.shape[1]
    total = times_columns(1, where_ref[2] % 2, left, columns.ready(), count)
    cross_ref[...] = -total
    factors = [split(total), split(own.ready()[...])]
    last_half(1, where_ref, p_rows, f_rows, factors, other_ref)


def last_mine(where_ref, cross_ref, p_rows, f_rows, own, mine_ref):
    factors = [split(-cross_ref[...]), split(own.ready()[...])]
    last_half(0, where_ref, p_rows, f_rows, factors, mine_ref)


def add_pieces(mine_ref, got_ref, *out_refs):
    for step, out_ref in enumerate(out_refs):
        out_ref[...] = mine_ref[step] + got_ref[step]


def finish(*refs):
    *in_refs, out_ref, turned_ref = refs
    total = sum(ref[...] for ref in in_refs)
    out_ref[...] = total
    turned_ref[...] = total.T


def local(top_factor, panel_two, panel_three, panel_four, factor_two, factor_three, factor_four):
    leaves = lax.axis_size("leaf")
    fronts = lax.axis_size("front")
    share = top_factor.shape[0]
    width = panel_four.shape[1]
    leaf = lax.axis_index("leaf")
    front = lax.axis_index("front")
    z, x, core = leaf // Y, front // CORES, front % CORES
    where = jnp.stack([x, core, z % 8]).astype(jnp.int32)
    y_groups = [list(range(i, i + Y)) for i in range(0, leaves, Y)]

    def from_plane(value, distance):
        pairs = [(i, ((i // Y) ^ distance) * Y + i % Y) for i in range(leaves)]
        return lax.ppermute(value, "leaf", pairs)

    def from_core(value):
        return lax.ppermute(value, "front", [(i, i ^ 1) for i in range(fronts)])

    def shift_x(value, distance):
        pairs = [
            (i, (i // CORES + distance) % XS * CORES + i % CORES) for i in range(fronts)
        ]
        return lax.ppermute(value, "front", pairs)

    def y_gather(value):
        return lax.all_gather(value, "leaf", axis=0, axis_index_groups=y_groups)

    stack = functools.partial(jax.ShapeDtypeStruct, dtype=jnp.float32)
    tile, tiles = stack((share, width)), stack((XS, share, width))
    def near_by(value):
        return ("near", value)

    def in_hbm(value):
        return ("hbm", value)

    def staged(value, *index):
        index = index or (slice(None),) * value.ndim
        part = jax.eval_shape(lambda v: v[index], value)
        return ("staged", value, index, part)

    def call(kernel, out_shape, flops, *inputs, hbm_outs=(), semaphores=0):
        specs, arrays, scratch = [], [], []
        for kind, value, *rest in inputs:
            arrays.append(value)
            if kind == "near":
                specs.append(pl.BlockSpec(value.shape, lambda i, n=value.ndim: (0,) * n))
            elif kind == "smem":
                specs.append(pl.BlockSpec(memory_space=pltpu.SMEM))
            else:
                specs.append(pl.BlockSpec(memory_space=pltpu.HBM))
            if kind == "staged":
                scratch.append(pltpu.VMEM(rest[1].shape, rest[1].dtype))
        count = len(scratch)
        scratch.append(pltpu.SemaphoreType.DMA((count + 1,)))
        if semaphores:
            scratch.append(pltpu.SemaphoreType.DMA((semaphores,)))

        def body(*refs):
            ins, rest = list(refs[: len(inputs)]), refs[len(inputs) :]
            outs, rest = rest[: len(out_shape)], rest[len(out_shape) :]
            parts, sems, more = rest[:count], rest[count], rest[count + 1 :]
            at = 0
            for index, (kind, *entry) in enumerate(inputs):
                if kind == "staged":
                    ins[index] = Staged(ins[index], entry[1], parts[at], sems.at[at])
                    at += 1
            kernel(*ins, *outs, *more)
            for value in ins:
                if isinstance(value, Staged):
                    value.ready()

        out_specs = [
            pl.BlockSpec(memory_space=pltpu.HBM)
            if index in hbm_outs
            else pl.BlockSpec(o.shape, lambda i, n=len(o.shape): (0,) * n)
            for index, o in enumerate(out_shape)
        ]
        return pl.pallas_call(
            body,
            out_shape=out_shape,
            grid=(1,),
            in_specs=specs,
            out_specs=out_specs,
            scratch_shapes=scratch,
            compiler_params=pltpu.CompilerParams(vmem_limit_bytes=VMEM_BYTES),
            cost_estimate=pl.CostEstimate(
                flops=flops, bytes_accessed=8_000_000, transcendentals=0
            ),
        )(*arrays)

    def front_total(other, mine):
        got = from_core(other)
        piece = stack(mine.shape[1:])
        pieces = call(add_pieces, [piece] * XS, 1_000_000, near_by(mine), near_by(got))
        parts = [pieces[0]] + [shift_x(pieces[d], d) for d in (1, 3, 2)]
        outs = [piece, stack(piece.shape[::-1])]
        outs = call(finish, outs, 1_000_000, *[near_by(part) for part in parts])
        return outs

    def plane_gather(parts):
        gathered = y_gather(jnp.stack(parts))
        return gathered.reshape(-1, *gathered.shape[2:])

    def padded(value):
        return jnp.pad(value, ((0, 0), (0, -value.shape[1] % 128)))

    panels = jnp.concatenate([padded(panel_three), padded(panel_two)], 1)
    panels = lax.all_gather(panels, "front", axis=0)
    lanes = slice(None), slice(None)
    where = ("smem", where)

    half = share // 2
    first = top_factor.T
    (two,) = call(
        turn,
        [stack((half, 2 * share))],
        1_000_000,
        staged(factor_two),
        staged(first),
        near_by(from_plane(first, 4)),
    )
    (near,) = call(
        pack,
        [stack((half, 6 * share))],
        1_000_000,
        near_by(two),
        near_by(from_plane(two, 2)),
        staged(factor_three),
    )
    f1, deep = call(
        join,
        [tile, stack((2, share, width))],
        1_000_000,
        where,
        near_by(near),
        near_by(from_plane(near, 1)),
        in_hbm(panels),
    )
    rows = y_gather(deep)
    f1_rows = y_gather(f1)

    work = 6 * share * share * XS * width
    count = panel_two.shape[1]
    inner, turned = call(
        top_product,
        [stack((share, count)), stack((count, share))],
        work // 4,
        staged(f1_rows),
        staged(panels, *lanes, slice(256, 384)),
    )
    p4, inner = lax.optimization_barrier((panel_four, inner))
    last_panel = lax.all_gather(p4, "front", axis=0)
    a_rows = plane_gather([turned] + [from_plane(turned, d) for d in (2, 1, 3)])
    b, g, turned = call(
        next_products,
        [stack((share, share))] * 2 + [stack((2, share, share))],
        work,
        where,
        staged(a_rows),
        staged(rows, slice(None), 0),
        staged(panels, *lanes, slice(0, 256)),
    )
    last, b = lax.optimization_barrier((jnp.stack([panel_four, factor_four]), b))
    last_rows = y_gather(last)
    got = from_plane(turned, 1)
    b_rows, g_rows = (plane_gather([turned[i], got[i]]) for i in range(2))

    half_sums = stack((XS, share, share))
    third = [
        where,
        near_by(b),
        near_by(g),
        staged(b_rows),
        staged(g_rows),
        staged(rows, slice(None), 1),
        staged(factor_three),
    ]
    other, mine = (
        call(functools.partial(third_terms, flip), [half_sums], work, *third)[0]
        for flip in (1, 0)
    )
    cov_three, turned = front_total(other, mine)

    widths = [top_factor.shape[1], count, count, share]
    (early,) = call(
        early_terms,
        [stack((fronts, share, sum(widths)))],
        2 * work,
        where,
        staged(f1_rows),
        staged(first),
        staged(inner),
        staged(a_rows),
        staged(rows, slice(None), 0),
        staged(factor_two),
        staged(b),
        staged(g),
    )
    early, turned = lax.optimization_barrier((early, turned))
    early = early.reshape(fronts * share, -1)
    early = lax.psum_scatter(early, "front", scatter_dimension=0, tiled=True)
    cuts = [stack((widths[0], share))] + [stack((share, w)) for w in widths[1:]]
    cov_one, cross_two, cov_two, cross_three = call(cut, cuts, 1_000_000, near_by(early))

    parent_rows = plane_gather([turned, from_plane(turned, 1)])
    last = [
        staged(last_rows, slice(None), 0),
        staged(last_rows, slice(None), 1),
        staged(factor_four),
    ]
    cross_four, other = call(
        last_other,
        [tile, tiles],
        2 * work,
        where,
        staged(parent_rows),
        staged(last_panel),
        *last,
    )
    (mine,) = call(last_mine, [tiles], work, where, near_by(cross_four), *last)
    cov_four, _ = front_total(other, mine)
    return cov_one.T, cross_two, cov_two, cross_three, cov_three, cross_four, cov_four


def solution(mesh):
    spec = P("front", "leaf")
    return jax.shard_map(
        local, mesh=mesh, in_specs=(spec,) * 7, out_specs=(spec,) * 7, check_vma=False
    )
```

```python
import functools

import jax
import jax.numpy as jnp
from jax import lax
from jax.experimental import pallas as pl
from jax.experimental.pallas import tpu as pltpu
from jax.sharding import PartitionSpec as P

Y = 4
XS = 4
CORES = 2
VMEM_BYTES = 52 * 1024 * 1024
VMEM_SMALL = 16 * 1024 * 1024


class Staged:

    def __init__(self, source, index, scratch, semaphore):
        self.copy = pltpu.make_async_copy(source.at[index], scratch, semaphore)
        self.scratch, self.waited = scratch, False
        self.copy.start()

    def ready(self):
        if not self.waited:
            self.copy.wait()
            self.waited = True
        return self.scratch


def split(value):
    high = value.astype(jnp.bfloat16)
    low = (value - high.astype(jnp.float32)).astype(jnp.bfloat16)
    return high, low


def product(first, second):
    (fh, fl), (sh, sl) = first, second
    run = functools.partial(jnp.dot, preferred_element_type=jnp.float32)
    return run(fh, sh) + (run(fh, sl) + run(fl, sh))


def block_of(ref, index):
    return ref[:, index * 176 : (index + 1) * 176]


def turn(f2, own, got_ref, out_ref):
    top = jnp.concatenate([own.ready()[...], got_ref[...]], 0)
    out_ref[...] = jnp.concatenate([f2.ready()[...].T, top], 1)


def pack(two_ref, got_ref, f3, out_ref):
    turned = f3.ready()[...].T
    parts = [two_ref[...], got_ref[...], turned[:88], turned[88:]]
    out_ref[...] = jnp.concatenate(parts, 1)


def join(where_ref, own_ref, got_ref, panels_ref, f1_ref, rows_ref):
    del panels_ref
    z = where_ref[2]

    def at(which, distance):
        far = ((distance >> 1) & 1) == 1
        own = jnp.where(far, block_of(own_ref, which + 2), block_of(own_ref, which))
        got = jnp.where(far, block_of(got_ref, which + 2), block_of(got_ref, which))
        return jnp.where((distance & 1) == 1, got, own)

    pieces = []
    for plane in range(8):
        distance = plane ^ z
        both = at(1, distance)
        pieces.append(jnp.where((distance >> 2) == 1, both[44:], both[:44]))
    f1_ref[...] = jnp.concatenate(pieces, 0).T
    pieces = [at(0, plane ^ (z % 4)) for plane in range(4)]
    rows_ref[0] = jnp.concatenate(pieces, 0).T
    pieces = []
    for plane in range(2):
        near = plane == (z % 2)
        for index in (4, 5):
            pieces.append(
                jnp.where(near, block_of(own_ref, index), block_of(got_ref, index))
            )
    rows_ref[1] = jnp.concatenate(pieces, 0).T


def sums(planes, turned, factors):
    for y in range(Y):
        total = None
        for tile, factor in zip(turned, factors):
            term = product(split(tile(y)), factor)
            total = term if total is None else total + term
        width = total.shape[0] // planes
        step = min(width, 176)
        for plane in range(planes):
            for part in range(0, width, step):
                column = (plane * Y + y) * width + part
                value = total[plane * width + part : plane * width + part + step]
                yield column // 176, slice(column % 176, column % 176 + step), value


def times_columns(planes, distances, left, columns_ref, count):
    total = None
    for y in range(Y):
        if planes == 4:
            parts = [
                columns_ref[p, y * 44 : (y + 1) * 44, :count] for p in range(8)
            ]
        elif planes == 2:
            low = (y % 2) * 88
            parts = []
            for q in range(4):
                p = distances ^ ((q & 1) * 2 + (q >> 1)) if distances is not None else q
                parts.append(columns_ref[p * 2 + y // 2, low : low + 88, :count])
        else:
            parts = [columns_ref[(distances ^ q) * Y + y, :, :count] for q in range(2)]
        term = product(split(left(y)), split(jnp.concatenate(parts, 0)))
        total = term if total is None else total + term
    return total


def top_product(rows, columns, out_ref, turned_ref):
    left = rows.ready()
    total = times_columns(4, None, lambda y: left[y], columns.ready(), out_ref.shape[1])
    out_ref[...] = total
    turned_ref[...] = total.T


def next_products(where_ref, a_rows, f2_rows, columns, b_ref, g_ref, turned_ref):
    count, z = b_ref.shape[1], where_ref[2]
    a, f2, right = a_rows.ready(), f2_rows.ready(), columns.ready()
    b = times_columns(2, None, lambda y: f2[y], right, count)
    g = times_columns(
        2, z % 4, lambda y: a[4 * y : 4 * y + 4].reshape(352, 176).T, right, count
    )
    b_ref[...], g_ref[...] = b, g
    turned_ref[0], turned_ref[1] = b.T, g.T


def pieces_of(ref, y, planes, z):
    pieces = []
    for plane in range(planes):
        distance = plane ^ (z % planes)
        at = distance if planes == 2 else (distance >> 1) + (distance & 1) * 2
        pieces.append(ref[y * planes + at])
    return jnp.concatenate(pieces, 0)


def third_terms(flip, where_ref, b_ref, g_ref, b_rows, g_rows, f3_rows, f3, out_ref):
    x, half, z = where_ref[0], where_ref[1] ^ flip, where_ref[2]
    factors = [split(b_ref[...]), split(g_ref[...]), split(f3.ready()[...])]
    for i in range(2):
        y = 2 * i + half
        turned = [
            pieces_of(b_rows.ready(), y, 2, z),
            pieces_of(g_rows.ready(), y, 2, z),
            f3_rows.ready()[y].T,
        ]
        total = sum(product(split(t), factor) for t, factor in zip(turned, factors))
        for plane in range(2):
            out_ref[(plane * 2 + i - x) % XS] = total[plane * 176 : plane * 176 + 176]


def early_terms(where_ref, f1_rows, f1, a, a_rows, f2_rows, f2, b, g, out_ref):
    z, inner = where_ref[2], a.ready()[...]
    factors = [split(jnp.concatenate([f1.ready()[...].T, -inner], 1))]
    first = factors[0][0].shape[1]
    for block, rows, value in sums(8, [lambda y: f1_rows.ready()[y].T], factors):
        out_ref[block, rows, :first] = value
    turned = [
        lambda y: pieces_of(a_rows.ready(), y, 4, z),
        lambda y: f2_rows.ready()[y].T,
    ]
    factors = [
        split(jnp.concatenate([inner, -g.ready()[...]], 1)),
        split(jnp.concatenate([f2.ready()[...], -b.ready()[...]], 1)),
    ]
    for block, rows, value in sums(4, turned, factors):
        out_ref[block, rows, first:] = value


def cut(early_ref, turned_ref, *out_refs):
    first, at = turned_ref.shape[0], turned_ref.shape[0]
    turned_ref[...] = early_ref[:, :first].T
    for out_ref in out_refs:
        out_ref[...] = early_ref[:, at : at + out_ref.shape[1]]
        at += out_ref.shape[1]


def last_half(flip, where_ref, p_rows, f_rows, factors, out_ref):
    x, half = where_ref[0], where_ref[1] ^ flip
    for y in range(Y):
        total = 0.0
        for rows, factor in zip((p_rows, f_rows), factors):
            tile = rows.ready()[y]
            tile = jnp.where(half == 0, tile[:, :176], tile[:, 176:])
            total += product(split(tile.T), factor)
        out_ref[(y - x) % XS] = total


def last_other(where_ref, parent, columns, p_rows, f_rows, own, cross_ref, other_ref):
    def left(y):
        return parent.ready()[2 * y : 2 * y + 2].reshape(352, 176).T

    count = cross_ref.shape[1]
    total = times_columns(1, where_ref[2] % 2, left, columns.ready(), count)
    cross_ref[...] = -total
    factors = [split(total), split(own.ready()[...])]
    last_half(1, where_ref, p_rows, f_rows, factors, other_ref)


def last_mine(where_ref, cross_ref, p_rows, f_rows, own, mine_ref):
    factors = [split(-cross_ref[...]), split(own.ready()[...])]
    last_half(0, where_ref, p_rows, f_rows, factors, mine_ref)


def add_pieces(mine_ref, got_ref, *out_refs):
    for step, out_ref in enumerate(out_refs):
        out_ref[...] = mine_ref[step] + got_ref[step]


def finish(*refs):
    *in_refs, out_ref, turned_ref = refs
    total = sum(ref[...] for ref in in_refs)
    out_ref[...] = total
    turned_ref[...] = total.T


def local(top_factor, panel_two, panel_three, panel_four, factor_two, factor_three, factor_four):
    leaves = lax.axis_size("leaf")
    fronts = lax.axis_size("front")
    share = top_factor.shape[0]
    width = panel_four.shape[1]
    leaf = lax.axis_index("leaf")
    front = lax.axis_index("front")
    z, x, core = leaf // Y, front // CORES, front % CORES
    where = jnp.stack([x, core, z % 8]).astype(jnp.int32)
    y_groups = [list(range(i, i + Y)) for i in range(0, leaves, Y)]

    def from_plane(value, distance):
        pairs = [(i, ((i // Y) ^ distance) * Y + i % Y) for i in range(leaves)]
        return lax.ppermute(value, "leaf", pairs)

    def from_core(value):
        return lax.ppermute(value, "front", [(i, i ^ 1) for i in range(fronts)])

    def shift_x(value, distance):
        pairs = [
            (i, (i // CORES + distance) % XS * CORES + i % CORES) for i in range(fronts)
        ]
        return lax.ppermute(value, "front", pairs)

    def y_gather(value):
        return lax.all_gather(value, "leaf", axis=0, axis_index_groups=y_groups)

    stack = functools.partial(jax.ShapeDtypeStruct, dtype=jnp.float32)
    tile, tiles = stack((share, width)), stack((XS, share, width))
    def near_by(value):
        return ("near", value)

    def in_hbm(value):
        return ("hbm", value)

    def staged(value, *index):
        index = index or (slice(None),) * value.ndim
        part = jax.eval_shape(lambda v: v[index], value)
        return ("staged", value, index, part)

    def call(kernel, out_shape, flops, *inputs, hbm_outs=(), semaphores=0):
        specs, arrays, scratch = [], [], []
        for kind, value, *rest in inputs:
            arrays.append(value)
            if kind == "near":
                specs.append(pl.BlockSpec(value.shape, lambda i, n=value.ndim: (0,) * n))
            elif kind == "smem":
                specs.append(pl.BlockSpec(memory_space=pltpu.SMEM))
            else:
                specs.append(pl.BlockSpec(memory_space=pltpu.HBM))
            if kind == "staged":
                scratch.append(pltpu.VMEM(rest[1].shape, rest[1].dtype))
        count = len(scratch)
        near_only = all(kind in ("near", "smem") for kind, *_ in inputs)
        limit = VMEM_SMALL if near_only else VMEM_BYTES
        scratch.append(pltpu.SemaphoreType.DMA((count + 1,)))
        if semaphores:
            scratch.append(pltpu.SemaphoreType.DMA((semaphores,)))

        def body(*refs):
            ins, rest = list(refs[: len(inputs)]), refs[len(inputs) :]
            outs, rest = rest[: len(out_shape)], rest[len(out_shape) :]
            parts, sems, more = rest[:count], rest[count], rest[count + 1 :]
            at = 0
            for index, (kind, *entry) in enumerate(inputs):
                if kind == "staged":
                    ins[index] = Staged(ins[index], entry[1], parts[at], sems.at[at])
                    at += 1
            kernel(*ins, *outs, *more)
            for value in ins:
                if isinstance(value, Staged):
                    value.ready()

        out_specs = [
            pl.BlockSpec(memory_space=pltpu.HBM)
            if index in hbm_outs
            else pl.BlockSpec(o.shape, lambda i, n=len(o.shape): (0,) * n)
            for index, o in enumerate(out_shape)
        ]
        return pl.pallas_call(
            body,
            out_shape=out_shape,
            grid=(1,),
            in_specs=specs,
            out_specs=out_specs,
            scratch_shapes=scratch,
            compiler_params=pltpu.CompilerParams(vmem_limit_bytes=limit),
            cost_estimate=pl.CostEstimate(
                flops=flops, bytes_accessed=8_000_000, transcendentals=0
            ),
        )(*arrays)

    def front_total(other, mine):
        got = from_core(other)
        piece = stack(mine.shape[1:])
        pieces = call(add_pieces, [piece] * XS, 1_000_000, near_by(mine), near_by(got))
        parts = [pieces[0]] + [shift_x(pieces[d], d) for d in (1, 3, 2)]
        outs = [piece, stack(piece.shape[::-1])]
        outs = call(finish, outs, 1_000_000, *[near_by(part) for part in parts])
        return outs

    def plane_gather(parts):
        gathered = y_gather(jnp.stack(parts))
        return gathered.reshape(-1, *gathered.shape[2:])

    def padded(value):
        return jnp.pad(value, ((0, 0), (0, -value.shape[1] % 128)))

    panels = jnp.concatenate([padded(panel_three), padded(panel_two)], 1)
    panels = lax.all_gather(panels, "front", axis=0)
    lanes = slice(None), slice(None)
    where = ("smem", where)

    half = share // 2
    first = top_factor.T
    (two,) = call(
        turn,
        [stack((half, 2 * share))],
        1_000_000,
        staged(factor_two),
        staged(first),
        near_by(from_plane(first, 4)),
    )
    (near,) = call(
        pack,
        [stack((half, 6 * share))],
        1_000_000,
        near_by(two),
        near_by(from_plane(two, 2)),
        staged(factor_three),
    )
    f1, deep = call(
        join,
        [tile, stack((2, share, width))],
        1_000_000,
        where,
        near_by(near),
        near_by(from_plane(near, 1)),
        in_hbm(panels),
    )
    rows = y_gather(deep)
    f1_rows = y_gather(f1)

    work = 6 * share * share * XS * width
    count = panel_two.shape[1]
    inner, turned = call(
        top_product,
        [stack((share, count)), stack((count, share))],
        work // 4,
        staged(f1_rows),
        staged(panels, *lanes, slice(256, 384)),
    )
    p4, inner = lax.optimization_barrier((panel_four, inner))
    last_panel = lax.all_gather(p4, "front", axis=0)
    a_rows = plane_gather([turned] + [from_plane(turned, d) for d in (2, 1, 3)])
    b, g, turned = call(
        next_products,
        [stack((share, share))] * 2 + [stack((2, share, share))],
        work,
        where,
        staged(a_rows),
        staged(rows, slice(None), 0),
        staged(panels, *lanes, slice(0, 256)),
    )
    last, b = lax.optimization_barrier((jnp.stack([panel_four, factor_four]), b))
    last_rows = y_gather(last)
    got = from_plane(turned, 1)
    b_rows, g_rows = (plane_gather([turned[i], got[i]]) for i in range(2))

    half_sums = stack((XS, share, share))
    third = [
        where,
        near_by(b),
        near_by(g),
        staged(b_rows),
        staged(g_rows),
        staged(rows, slice(None), 1),
        staged(factor_three),
    ]
    other, mine = (
        call(functools.partial(third_terms, flip), [half_sums], work, *third)[0]
        for flip in (1, 0)
    )
    cov_three, turned = front_total(other, mine)

    widths = [top_factor.shape[1], count, count, share]
    (early,) = call(
        early_terms,
        [stack((fronts, share, sum(widths)))],
        2 * work,
        where,
        staged(f1_rows),
        staged(first),
        staged(inner),
        staged(a_rows),
        staged(rows, slice(None), 0),
        staged(factor_two),
        staged(b),
        staged(g),
    )
    early, turned = lax.optimization_barrier((early, turned))
    early = early.reshape(fronts * share, -1)
    early = lax.psum_scatter(early, "front", scatter_dimension=0, tiled=True)
    cuts = [stack((widths[0], share))] + [stack((share, w)) for w in widths[1:]]
    cov_one, cross_two, cov_two, cross_three = call(cut, cuts, 1_000_000, near_by(early))

    parent_rows = plane_gather([turned, from_plane(turned, 1)])
    last = [
        staged(last_rows, slice(None), 0),
        staged(last_rows, slice(None), 1),
        staged(factor_four),
    ]
    cross_four, other = call(
        last_other,
        [tile, tiles],
        2 * work,
        where,
        staged(parent_rows),
        staged(last_panel),
        *last,
    )
    (mine,) = call(last_mine, [tiles], work, where, near_by(cross_four), *last)
    cov_four, _ = front_total(other, mine)
    return cov_one.T, cross_two, cov_two, cross_three, cov_three, cross_four, cov_four


def solution(mesh):
    spec = P("front", "leaf")
    return jax.shard_map(
        local, mesh=mesh, in_specs=(spec,) * 7, out_specs=(spec,) * 7, check_vma=False
    )
```
